32 devices in a mesh: row: 4 (over z), col: 8 (over y, x, core).
Axes of the slice: x: 2, y: 2, z: 4, core: 2. Of those that a mesh axis runs over, the one named last changes fastest.
Arguments:
- children: float32 [2, 1024, 4096], P(None, 'row', 'col'), may hold values from -1 to 6, as said below
- block_maps: int32 [2, 16], replicated, may hold values from 0 to 15, each once within a row
Outputs:
- panel_rows: float32 [512, 4096], P(None, 'col')
- trailing: float32 [2, 1024, 4096], P(None, 'row', 'col')
The draws below stay inside these ranges and needn't reach their ends.
Inputs may be any that keep to these rules, and one draw needn't show every extreme that they name: Each row of block_maps names every parent column block once. `children`: each child's block is upper triangular in its own column order: entry (i, j) is zero where j < i.
All inputs are finite; a program needn't handle non-finite values.
Results may differ from the reference program's by a relative error of at most 0.000078.
Values sent between devices are 32-bit elements; how exact they have to be, the bound alone decides.
No kernel may reach another device: no remote copies, remote signals or barrier semaphores. Data moves between devices by JAX's collectives and lax.ppermute only.
A program may use at most 64 MiB of HBM per device.

```python
import jax
import jax.numpy as jnp
from jax import lax

PANEL = 256
CROWS = 1024
NBLK = 16
NP = 4096


def draw_children(key, part):
    key_off, key_diag = jax.random.split(key, 2)
    row_index = jnp.arange(CROWS, dtype=jnp.int32)[None, :, None]
    col_index = jnp.arange(NP, dtype=jnp.int32)[None, None, :]
    offdiag = jnp.clip(0.15 * jax.random.normal(key_off, (2, CROWS, NP), jnp.float32), -0.9, 0.9)
    diagonal = jax.random.uniform(key_diag, (2, CROWS, 1), jnp.float32, 3.0, 6.0)
    upper = jnp.where(col_index > row_index, offdiag, 0.0)
    return jnp.where(col_index == row_index, diagonal, upper).astype(jnp.float32)


def setup_inputs(seed: int = 0) -> dict:
    arg_keys = jax.random.split(jax.random.key(seed), 3)
    return {
        "children": draw_children(jax.random.fold_in(arg_keys[2], 71), 0),
        "block_maps": jax.vmap(lambda own: jax.random.permutation(own, NBLK))(jax.random.split(arg_keys[1], 2)).reshape((2, NBLK)).astype(jnp.int32),
    }


def crossed(left_matrix, right_matrix):
    return jnp.dot(left_matrix.T.astype(jnp.float32), right_matrix.astype(jnp.float32), precision=lax.Precision.HIGHEST, preferred_element_type=jnp.float32)

def applied(left_matrix, right_matrix):
    return jnp.dot(left_matrix.astype(jnp.float32), right_matrix.astype(jnp.float32), precision=lax.Precision.HIGHEST, preferred_element_type=jnp.float32)

def orthonormal(panel_cols):
    factor = jnp.linalg.cholesky(crossed(panel_cols, panel_cols))
    return lax.linalg.triangular_solve(factor, panel_cols, left_side=False, lower=True, transpose_a=True)

def placed(child_rows, mapping):
    block_count = NP // PANEL
    inverse = jnp.zeros((block_count,), jnp.int32).at[mapping].set(jnp.arange(block_count, dtype=jnp.int32))
    blocks = child_rows.reshape(CROWS, block_count, PANEL)
    return jnp.take(blocks, inverse, axis=1).reshape(CROWS, NP)

def reference(children, block_maps):
    front = jnp.concatenate([placed(children[0], block_maps[0]), placed(children[1], block_maps[1])], axis=0)
    basis_one = orthonormal(front[:, :PANEL])
    rows_one = crossed(basis_one, front)
    front = front - applied(basis_one, rows_one)
    basis_two = orthonormal(front[:, PANEL:2 * PANEL])
    rows_two = crossed(basis_two, front)
    front = front - applied(basis_two, rows_two)
    return (jnp.concatenate([rows_one, rows_two], axis=0), front.reshape(2, CROWS, NP))
```

```python
import jax
import jax.numpy as jnp
from jax import lax
from jax.sharding import PartitionSpec as P

PANEL = 256
LANES = 128


def dot(left, right, contract):
    return lax.dot_general(
        left,
        right,
        (contract, ((), ())),
        precision=lax.Precision.HIGHEST,
        preferred_element_type=jnp.float32,
    )


def pairs_xor(size, mask):
    return [(i, i ^ mask) for i in range(size)]


def gather_col(piece, size):
    even = [piece] + [lax.ppermute(piece, "col", pairs_xor(size, k)) for k in range(2, size, 2)]
    near = jnp.stack(even)
    far = lax.ppermute(near, "col", pairs_xor(size, 1))
    return jnp.stack([near, far], axis=1).reshape((size,) + piece.shape)


def by_position(pieces, size):
    me = lax.axis_index("col")
    return jnp.take(pieces, jnp.arange(size, dtype=jnp.int32) ^ me, axis=0)


def sum_row_small(value, size):
    span = 2
    while span <= size:
        value = value + lax.ppermute(value, "row", pairs_xor(size, span - 1))
        span *= 2
    return value


def sum_row_chain(value, size):
    place = lax.axis_index("row")
    half = size // 2
    for hop in range(half - 1):
        value = value + lax.ppermute(
            value, "row", [(hop, hop + 1), (size - 1 - hop, size - 2 - hop)]
        )
    value = value + lax.ppermute(value, "row", [(half - 1, half), (half, half - 1)])
    for hop in range(half - 1):
        low, high = half - 1 - hop, half + hop
        came = lax.ppermute(value, "row", [(low, low - 1), (high, high + 1)])
        value = jnp.where((place == low - 1) | (place == high + 1), came, value)
    return value


def inverted(mapping, block_count):
    return (
        jnp.zeros((block_count,), jnp.int32)
        .at[mapping]
        .set(jnp.arange(block_count, dtype=jnp.int32))
    )


def per_device(children, block_maps):
    cols = lax.axis_size("col")
    rows = lax.axis_size("row")
    me = lax.axis_index("col")
    rows_dev, width = children.shape[1], children.shape[2]
    blocks_dev = width // PANEL
    block_count = blocks_dev * cols
    part = rows_dev // cols
    inverse = jnp.stack([inverted(block_maps[c], block_count) for c in range(2)])

    outgoing = children.reshape(2, cols, part, width).transpose(1, 0, 2, 3)
    spread = lax.all_to_all(outgoing, "col", 0, 0, tiled=True)
    blocks = spread.reshape(cols, 2, part, blocks_dev, PANEL).transpose(1, 0, 3, 2, 4)
    blocks = blocks.reshape(2, block_count, part, PANEL)
    ordered = jnp.stack([jnp.take(blocks[c], inverse[c], axis=0) for c in range(2)])
    ordered = ordered.reshape(2, cols, blocks_dev, part, PANEL)

    both = 2 * PANEL
    mine = ordered[:, 0].transpose(0, 2, 1, 3).reshape(2 * part, both)
    pieces = gather_col(mine, cols)
    panels = by_position(pieces, cols).reshape(cols * 2 * part, both)

    onward = ordered.transpose(1, 0, 3, 2, 4)
    settled = lax.all_to_all(onward, "col", 0, 0, tiled=True)
    front = settled.reshape(cols * 2 * part, width)

    groups = cols // (both // LANES)
    height = both // groups
    left = lax.dynamic_slice_in_dim(panels, (me % groups) * height, height, axis=1)
    right = lax.dynamic_slice_in_dim(panels, (me // groups) * LANES, LANES, axis=1)
    tile = sum_row_small(dot(left, right, ((0,), (0,))), rows)
    tiles = by_position(gather_col(tile, cols), cols)
    gram = tiles.reshape(both // LANES, groups, height, LANES).transpose(1, 2, 0, 3)
    gram = gram.reshape(both, both)

    factor = jnp.linalg.cholesky(gram)
    inv = lax.linalg.triangular_solve(
        factor, jnp.eye(both, dtype=jnp.float32), left_side=True, lower=True
    )
    basis = dot(panels, inv, ((1,), (1,)))

    outs, fronts = [], []
    for b in range(blocks_dev):
        block = front[:, b * PANEL : (b + 1) * PANEL]
        summed = [
            sum_row_chain(dot(panels[:, p * PANEL : (p + 1) * PANEL], block, ((0,), (0,))), rows)
            for p in range(2)
        ]
        upper = dot(inv, jnp.concatenate(summed, axis=0), ((1,), (0,)))
        outs.append(upper)
        fronts.append(block - dot(basis, upper, ((1,), (0,))))
    upper_rows = jnp.concatenate(outs, axis=1)
    result = jnp.concatenate(fronts, axis=1).reshape(cols, 2, part, width)
    result = result.transpose(1, 0, 2, 3).reshape(2, rows_dev, width)
    return (upper_rows, result)


def solution(mesh):
    placed = (P(None, "row", "col"), P())
    return jax.shard_map(
        per_device,
        mesh=mesh,
        in_specs=placed,
        out_specs=(P(None, "col"), P(None, "row", "col")),
        check_vma=False,
    )
```

```python
import jax
import jax.numpy as jnp
from jax import lax
from jax.experimental import pallas as pl
from jax.experimental.pallas import tpu as pltpu
from jax.sharding import PartitionSpec as P

PANEL = 256
LANES = 128
SUBS = 8


def dot(left, right, contract):
    return lax.dot_general(
        left,
        right,
        (contract, ((), ())),
        precision=lax.Precision.HIGHEST,
        preferred_element_type=jnp.float32,
    )


def row_of(x, i):
    return jnp.broadcast_to(x[i : i + 1, :], (SUBS, LANES))


def column_of(x, j):
    return jnp.broadcast_to(x[:, j : j + 1], (SUBS, LANES))


def combined(weights, rows):
    p = [w * r for w, r in zip(weights, rows)]
    return ((p[0] + p[1]) + (p[2] + p[3])) + ((p[4] + p[5]) + (p[6] + p[7]))


def small_inverse(cols):
    sub = lax.broadcasted_iota(jnp.int32, (SUBS, LANES), 0)
    x = list(cols)
    t = [jnp.zeros((SUBS, LANES), jnp.float32) for _ in range(SUBS)]
    for j in range(SUBS):
        pivot = row_of(x[j], j)
        reciprocal = 1.0 / pivot
        root = lax.rsqrt(pivot)
        here = sub == j
        xj = x[j]
        for k in range(SUBS):
            if k == j:
                continue
            b = row_of(x[k], j)
            if k < j:
                t[k] = jnp.where(here, root * b, t[k])
            b = b * reciprocal
            x[k] = jnp.where(here, b, x[k] - xj * b)
        t[j] = jnp.where(here, root, t[j])
        x[j] = jnp.where(here, reciprocal, -xj * reciprocal)
    return x, t


def factor_inverse(block):
    steps = LANES // SUBS
    lane = lax.broadcasted_iota(jnp.int32, (SUBS, LANES), 1)
    sub = lax.broadcasted_iota(jnp.int32, (SUBS, LANES), 0)
    a = [block[SUBS * i : SUBS * (i + 1), :] for i in range(steps)]
    e = [jnp.where(lane == sub + SUBS * i, 1.0, 0.0).astype(jnp.float32) for i in range(steps)]
    out = []
    for s in range(steps):
        inv, t = small_inverse([column_of(a[s], SUBS * s + k) for k in range(SUBS)])
        rows_a = [row_of(a[s], k) for k in range(SUBS)]
        rows_e = [row_of(e[s], k) for k in range(SUBS)]
        out.append(combined(t, rows_e))
        if s + 1 < steps:
            scaled_a, scaled_e = combined(inv, rows_a), combined(inv, rows_e)
            scaled_a = [row_of(scaled_a, k) for k in range(SUBS)]
            scaled_e = [row_of(scaled_e, k) for k in range(SUBS)]
            for i in range(s + 1, steps):
                c = [column_of(a[i], SUBS * s + k) for k in range(SUBS)]
                a[i] = a[i] - combined(c, scaled_a)
                e[i] = e[i] - combined(c, scaled_e)
    return jnp.concatenate(out, 0)


def cholesky_inverse_kernel(gram_ref, out_ref, a_ref):
    size = gram_ref.shape[0]
    a_ref[...] = gram_ref[...]
    out_ref[...] = jnp.zeros_like(out_ref)
    for lo in range(0, size, LANES):
        hi = lo + LANES
        inv = factor_inverse(a_ref[lo:hi, lo:hi])
        if lo > 0:
            out_ref[lo:hi, :lo] = dot(inv, out_ref[lo:hi, :lo], ((1,), (0,)))
        out_ref[lo:hi, lo:hi] = inv
        if hi < size:
            right = dot(inv, a_ref[lo:hi, hi:], ((1,), (0,)))
            a_ref[hi:, hi:] = a_ref[hi:, hi:] - dot(right, right, ((0,), (0,)))
            out_ref[hi:, :hi] = out_ref[hi:, :hi] - dot(right, out_ref[lo:hi, :hi], ((0,), (0,)))


def cholesky_inverse(gram):
    size = gram.shape[0]
    return pl.pallas_call(
        cholesky_inverse_kernel,
        out_shape=jax.ShapeDtypeStruct((size, size), jnp.float32),
        in_specs=[pl.BlockSpec(memory_space=pltpu.VMEM)],
        out_specs=pl.BlockSpec(memory_space=pltpu.VMEM),
        scratch_shapes=[pltpu.VMEM((size, size), jnp.float32)],
        compiler_params=pltpu.CompilerParams(vmem_limit_bytes=32 << 20),
        cost_estimate=pl.CostEstimate(
            flops=20_000_000_000, bytes_accessed=8 * size * size, transcendentals=size
        ),
    )(gram)


def pairs_xor(size, mask):
    return [(i, i ^ mask) for i in range(size)]


def gather_col(piece, size):
    even = [piece] + [lax.ppermute(piece, "col", pairs_xor(size, k)) for k in range(2, size, 2)]
    near = jnp.stack(even)
    far = lax.ppermute(near, "col", pairs_xor(size, 1))
    return jnp.stack([near, far], axis=1).reshape((size,) + piece.shape)


def by_position(pieces, size):
    me = lax.axis_index("col")
    return jnp.take(pieces, jnp.arange(size, dtype=jnp.int32) ^ me, axis=0)


def sum_row_small(value, size):
    span = 2
    while span <= size:
        value = value + lax.ppermute(value, "row", pairs_xor(size, span - 1))
        span *= 2
    return value


def sum_row_chain(value, size):
    place = lax.axis_index("row")
    half = size // 2
    for hop in range(half - 1):
        value = value + lax.ppermute(
            value, "row", [(hop, hop + 1), (size - 1 - hop, size - 2 - hop)]
        )
    value = value + lax.ppermute(value, "row", [(half - 1, half), (half, half - 1)])
    for hop in range(half - 1):
        low, high = half - 1 - hop, half + hop
        came = lax.ppermute(value, "row", [(low, low - 1), (high, high + 1)])
        value = jnp.where((place == low - 1) | (place == high + 1), came, value)
    return value


def inverted(mapping, block_count):
    return (
        jnp.zeros((block_count,), jnp.int32)
        .at[mapping]
        .set(jnp.arange(block_count, dtype=jnp.int32))
    )


def per_device(children, block_maps):
    cols = lax.axis_size("col")
    rows = lax.axis_size("row")
    me = lax.axis_index("col")
    rows_dev, width = children.shape[1], children.shape[2]
    blocks_dev = width // PANEL
    block_count = blocks_dev * cols
    part = rows_dev // cols
    inverse = jnp.stack([inverted(block_maps[c], block_count) for c in range(2)])

    outgoing = children.reshape(2, cols, part, width).transpose(1, 0, 2, 3)
    spread = lax.all_to_all(outgoing, "col", 0, 0, tiled=True)
    blocks = spread.reshape(cols, 2, part, blocks_dev, PANEL).transpose(1, 0, 3, 2, 4)
    blocks = blocks.reshape(2, block_count, part, PANEL)
    ordered = jnp.stack([jnp.take(blocks[c], inverse[c], axis=0) for c in range(2)])
    ordered = ordered.reshape(2, cols, blocks_dev, part, PANEL)

    both = 2 * PANEL
    mine = ordered[:, 0].transpose(0, 2, 1, 3).reshape(2 * part, both)
    pieces = gather_col(mine, cols)
    panels = by_position(pieces, cols).reshape(cols * 2 * part, both)

    onward = ordered.transpose(1, 0, 3, 2, 4)
    settled = lax.all_to_all(onward, "col", 0, 0, tiled=True)
    front = settled.reshape(cols * 2 * part, width)

    groups = cols // (both // LANES)
    height = both // groups
    left = lax.dynamic_slice_in_dim(panels, (me % groups) * height, height, axis=1)
    right = lax.dynamic_slice_in_dim(panels, (me // groups) * LANES, LANES, axis=1)
    tile = sum_row_small(dot(left, right, ((0,), (0,))), rows)
    tiles = by_position(gather_col(tile, cols), cols)
    gram = tiles.reshape(both // LANES, groups, height, LANES).transpose(1, 2, 0, 3)
    gram = gram.reshape(both, both)

    inv = cholesky_inverse(gram)
    basis = dot(panels, inv, ((1,), (1,)))

    outs, fronts = [], []
    for b in range(blocks_dev):
        block = front[:, b * PANEL : (b + 1) * PANEL]
        summed = [
            sum_row_chain(dot(panels[:, p * PANEL : (p + 1) * PANEL], block, ((0,), (0,))), rows)
            for p in range(2)
        ]
        upper = dot(inv, jnp.concatenate(summed, axis=0), ((1,), (0,)))
        outs.append(upper)
        fronts.append(block - dot(basis, upper, ((1,), (0,))))
    upper_rows = jnp.concatenate(outs, axis=1)
    result = jnp.concatenate(fronts, axis=1).reshape(cols, 2, part, width)
    result = result.transpose(1, 0, 2, 3).reshape(2, rows_dev, width)
    return (upper_rows, result)


def solution(mesh):
    placed = (P(None, "row", "col"), P())
    return jax.shard_map(
        per_device,
        mesh=mesh,
        in_specs=placed,
        out_specs=(P(None, "col"), P(None, "row", "col")),
        check_vma=False,
    )
```

```python
import jax
import jax.numpy as jnp
from jax import lax
from jax.experimental import pallas as pl
from jax.experimental.pallas import tpu as pltpu
from jax.sharding import PartitionSpec as P

PANEL = 256
LANES = 128
SUBS = 8
ANY = pl.BlockSpec(memory_space=pl.ANY)
VMEM = pl.BlockSpec(memory_space=pltpu.VMEM)
SMEM = pl.BlockSpec(memory_space=pltpu.SMEM)
KERNEL = pltpu.CompilerParams(vmem_limit_bytes=24 << 20)
F32 = jnp.float32


def dot(left, right, contract):
    return lax.dot_general(
        left,
        right,
        (contract, ((), ())),
        precision=lax.Precision.HIGHEST,
        preferred_element_type=F32,
    )


def shape(*dims):
    return jax.ShapeDtypeStruct(dims, F32)


def cost(flops, size):
    return pl.CostEstimate(flops=flops, bytes_accessed=size, transcendentals=0)


def run_copies(copies):
    for copy in copies:
        copy.start()
    for copy in copies:
        copy.wait()


def pack_kernel(children_ref, out_ref, sems):
    parts, _, part, _ = out_ref.shape
    run_copies(
        [
            pltpu.make_async_copy(
                children_ref.at[:, pl.ds(part * d, part), :], out_ref.at[d], sems.at[d]
            )
            for d in range(parts)
        ]
    )


def pack(children, parts):
    two, rows_dev, width = children.shape
    return pl.pallas_call(
        pack_kernel,
        out_shape=shape(parts, two, rows_dev // parts, width),
        in_specs=[ANY],
        out_specs=ANY,
        scratch_shapes=[pltpu.SemaphoreType.DMA((parts,))],
        compiler_params=KERNEL,
        cost_estimate=cost(0, 8 * children.size),
    )(children)


def order_kernel(maps_ref, spread_ref, out_ref, sems):
    owners, _, _, width = out_ref.shape
    per = width // PANEL
    copies = []
    for child in range(2):
        for block in range(owners * per):
            to = maps_ref[child, block]
            from_lane = (block % per) * PANEL
            to_lane = pl.multiple_of(lax.rem(to, per) * PANEL, PANEL)
            copies.append(
                pltpu.make_async_copy(
                    spread_ref.at[block // per, child, :, pl.ds(from_lane, PANEL)],
                    out_ref.at[lax.div(to, per), child, :, pl.ds(to_lane, PANEL)],
                    sems.at[child, block],
                )
            )
    run_copies(copies)


def order(spread, maps):
    return pl.pallas_call(
        order_kernel,
        out_shape=shape(*spread.shape),
        in_specs=[SMEM, ANY],
        out_specs=ANY,
        scratch_shapes=[pltpu.SemaphoreType.DMA(maps.shape)],
        compiler_params=KERNEL,
        cost_estimate=cost(0, 8 * spread.size),
    )(maps, spread)


def tile_kernel(near_ref, far_ref, panels_ref, tile_ref):
    me = lax.axis_index("col")
    half, part, both = near_ref.shape
    height = tile_ref.shape[0]
    groups = both // height
    for i in range(half):
        for ref, k in ((near_ref, 2 * i), (far_ref, 2 * i + 1)):
            at = pl.multiple_of(lax.bitwise_xor(me, k) * part, part)
            panels_ref[pl.ds(at, part), :] = ref[i]
    if height % LANES == 0:
        left = panels_ref[:, pl.ds(pl.multiple_of(lax.rem(me, groups) * height, height), height)]
    else:
        per = LANES // height
        group = lax.rem(me, groups)
        wide = panels_ref[:, pl.ds(pl.multiple_of(lax.div(group, per) * LANES, LANES), LANES)]
        left = wide[:, :height]
        for step in range(1, per):
            piece = wide[:, step * height : (step + 1) * height]
            left = jnp.where(lax.rem(group, per) == step, piece, left)
    right = panels_ref[:, pl.ds(pl.multiple_of(lax.div(me, groups) * LANES, LANES), LANES)]
    tile_ref[...] = dot(left, right, ((0,), (0,)))


def gram_tile(near, far):
    half, part, both = near.shape
    height = both * both // (2 * half * LANES)
    rows_dev = 2 * half * part
    return pl.pallas_call(
        tile_kernel,
        out_shape=(shape(rows_dev, both), shape(height, LANES)),
        in_specs=[VMEM, VMEM],
        out_specs=(VMEM, VMEM),
        compiler_params=KERNEL,
        cost_estimate=cost(12 * rows_dev * height * LANES, 12 * rows_dev * both),
    )(near, far)


def row_of(x, i):
    return jnp.broadcast_to(x[i : i + 1, :], (SUBS, LANES))


def column_of(x, j):
    return jnp.broadcast_to(x[:, j : j + 1], (SUBS, LANES))


def combined(weights, rows):
    p = [w * r for w, r in zip(weights, rows)]
    return ((p[0] + p[1]) + (p[2] + p[3])) + ((p[4] + p[5]) + (p[6] + p[7]))


def small_inverse(cols):
    sub = lax.broadcasted_iota(jnp.int32, (SUBS, LANES), 0)
    x = list(cols)
    t = [jnp.zeros((SUBS, LANES), F32) for _ in range(SUBS)]
    for j in range(SUBS):
        pivot = row_of(x[j], j)
        reciprocal = 1.0 / pivot
        root = lax.rsqrt(pivot)
        here = sub == j
        xj = x[j]
        for k in range(SUBS):
            if k == j:
                continue
            b = row_of(x[k], j)
            if k < j:
                t[k] = jnp.where(here, root * b, t[k])
            b = b * reciprocal
            x[k] = jnp.where(here, b, x[k] - xj * b)
        t[j] = jnp.where(here, root, t[j])
        x[j] = jnp.where(here, reciprocal, -xj * reciprocal)
    return x, t


def factor_inverse(block):
    steps = LANES // SUBS
    lane = lax.broadcasted_iota(jnp.int32, (SUBS, LANES), 1)
    sub = lax.broadcasted_iota(jnp.int32, (SUBS, LANES), 0)
    a = [block[SUBS * i : SUBS * (i + 1), :] for i in range(steps)]
    e = [jnp.where(lane == sub + SUBS * i, 1.0, 0.0).astype(F32) for i in range(steps)]
    out = []
    for s in range(steps):
        inv, t = small_inverse([column_of(a[s], SUBS * s + k) for k in range(SUBS)])
        rows_a = [row_of(a[s], k) for k in range(SUBS)]
        rows_e = [row_of(e[s], k) for k in range(SUBS)]
        out.append(combined(t, rows_e))
        if s + 1 < steps:
            scaled_a, scaled_e = combined(inv, rows_a), combined(inv, rows_e)
            scaled_a = [row_of(scaled_a, k) for k in range(SUBS)]
            scaled_e = [row_of(scaled_e, k) for k in range(SUBS)]
            for i in range(s + 1, steps):
                c = [column_of(a[i], SUBS * s + k) for k in range(SUBS)]
                a[i] = a[i] - combined(c, scaled_a)
                e[i] = e[i] - combined(c, scaled_e)
    return jnp.concatenate(out, 0)


def eliminate(lo, a_ref, out_ref):
    size, hi = a_ref.shape[0], lo + LANES
    inv = factor_inverse(a_ref[lo:hi, lo:hi])
    if lo > 0:
        out_ref[lo:hi, :lo] = dot(inv, out_ref[lo:hi, :lo], ((1,), (0,)))
    out_ref[lo:hi, lo:hi] = inv
    if hi < size:
        right = dot(inv, a_ref[lo:hi, hi:], ((1,), (0,)))
        a_ref[hi:, hi:] = a_ref[hi:, hi:] - dot(right, right, ((0,), (0,)))
        out_ref[hi:, :hi] = out_ref[hi:, :hi] - dot(right, out_ref[lo:hi, :hi], ((0,), (0,)))


def stage_kernel(index, adds, *refs):
    taken = refs[: 2 + 2 * adds]
    a_ref, out_ref = refs[2 + 2 * adds : 4 + 2 * adds]
    sums = refs[4 + 2 * adds : 4 + 3 * adds]
    landed, sems = refs[4 + 3 * adds :]
    copies = [
        pltpu.make_async_copy(taken[3 + 2 * i], landed.at[i], sems.at[i]) for i in range(adds)
    ]
    for copy in copies:
        copy.start()
    if index == 0:
        me = lax.axis_index("col")
        near_ref, far_ref = taken[:2]
        half, height, _ = near_ref.shape
        groups = a_ref.shape[0] // height
        for i in range(half):
            for ref, k in ((near_ref, 2 * i), (far_ref, 2 * i + 1)):
                at = lax.bitwise_xor(me, k)
                row = pl.multiple_of(lax.rem(at, groups) * height, height)
                lane = pl.multiple_of(lax.div(at, groups) * LANES, LANES)
                a_ref[pl.ds(row, height), pl.ds(lane, LANES)] = ref[i]
        out_ref[...] = jnp.zeros_like(out_ref)
    eliminate(index * LANES, a_ref, out_ref)
    for i, copy in enumerate(copies):
        copy.wait()
        sums[i][...] = taken[2 + 2 * i][...] + landed[i]


def stage(index, size, state, adds):
    flat = [ref for pair in adds for ref in pair]
    chunk = (PANEL, PANEL)
    outs = pl.pallas_call(
        lambda *refs: stage_kernel(index, len(adds), *refs),
        out_shape=[shape(size, size)] * 2 + [shape(*chunk)] * len(adds),
        in_specs=[VMEM, VMEM] + [VMEM, ANY] * len(adds),
        out_specs=[VMEM] * (2 + len(adds)),
        input_output_aliases={0: 0, 1: 1} if index > 0 else {},
        scratch_shapes=[
            pltpu.VMEM((max(len(adds), 1),) + chunk, F32),
            pltpu.SemaphoreType.DMA((max(len(adds), 1),)),
        ],
        compiler_params=KERNEL,
        cost_estimate=cost(6_000_000_000, 8 * size * size),
        name="factor",
    )(*state, *flat)
    return outs[:2], outs[2:]


def finish_kernel(index, inv_ref, basis_ref, front_ref, *refs):
    given = 6 if index > 0 else 4
    chunks = refs[:4]
    upper_ref, trail_ref, m_ref, w_ref, f_ref, sems = refs[given:]
    rows = lax.axis_size("row")
    place = lax.axis_index("row")
    outer = (place == 0) | (place == rows - 1)
    for p in range(2):
        own, came = chunks[2 * p], chunks[2 * p + 1]
        into = m_ref.at[pl.ds(PANEL * p, PANEL), :]

        @pl.when(outer)
        def _():
            pltpu.make_async_copy(came, into, sems.at[p]).start()

        @pl.when(jnp.logical_not(outer))
        def _():
            pltpu.make_async_copy(own, into, sems.at[p]).start()

    for p in range(2):
        into = m_ref.at[pl.ds(PANEL * p, PANEL), :]
        pltpu.make_async_copy(chunks[2 * p], into, sems.at[p]).wait()
    w_ref[...] = dot(inv_ref[...], m_ref[...], ((1,), (0,)))
    columns = pl.ds(PANEL * index, PANEL)
    upper_copy = pltpu.make_async_copy(w_ref, upper_ref.at[:, columns], sems.at[0])
    upper_copy.start()
    product = dot(basis_ref[...], w_ref[...], ((1,), (0,)))
    owners, two, part = front_ref.shape[:3]
    for owner in range(owners):
        for child in range(two):
            at = (owner * two + child) * part
            f_ref[child, owner * part : (owner + 1) * part, :] = (
                front_ref[owner, child, :, PANEL * index : PANEL * (index + 1)]
                - product[at : at + part, :]
            )
    trail_copy = pltpu.make_async_copy(f_ref, trail_ref.at[:, :, columns], sems.at[1])
    trail_copy.start()
    upper_copy.wait()
    trail_copy.wait()


def finish(index, inv, basis, front, chunks, given):
    owners, two, part, width = front.shape
    both = inv.shape[0]
    outs = (shape(both, width), shape(two, owners * part, width))
    return pl.pallas_call(
        lambda *refs: finish_kernel(index, *refs),
        out_shape=outs,
        in_specs=[VMEM, VMEM, VMEM] + [ANY] * (4 + len(given)),
        out_specs=(ANY, ANY),
        input_output_aliases={7: 0, 8: 1} if given else {},
        scratch_shapes=[
            pltpu.VMEM((both, PANEL), F32),
            pltpu.VMEM((both, PANEL), F32),
            pltpu.VMEM((two, owners * part, PANEL), F32),
            pltpu.SemaphoreType.DMA((2,)),
        ],
        compiler_params=KERNEL,
        cost_estimate=cost(24 * both * both * PANEL, 24 * both * PANEL),
        name="finish",
    )(inv, basis, front, *chunks, *given)


def pairs_xor(size, mask):
    return [(i, i ^ mask) for i in range(size)]


def gather_col(piece, size):
    even = [piece] + [lax.ppermute(piece, "col", pairs_xor(size, k)) for k in range(2, size, 2)]
    near = jnp.stack(even)
    return near, lax.ppermute(near, "col", pairs_xor(size, 1))


def sum_row_small(value, size):
    span = 2
    while span <= size:
        value = value + lax.ppermute(value, "row", pairs_xor(size, span - 1))
        span *= 2
    return value


def inwards(value, size):
    for hop in range(size // 2 - 1):
        came = lax.ppermute(value, "row", [(hop, hop + 1), (size - 1 - hop, size - 2 - hop)])
        if hop == size // 2 - 2:
            return value, came
        value = value + came


def across(value, size):
    half = size // 2
    return value, lax.ppermute(value, "row", [(half - 1, half), (half, half - 1)])


def outwards(value, size):
    half = size // 2
    place = lax.axis_index("row")
    for hop in range(half - 1):
        low, high = half - 1 - hop, half + hop
        came = lax.ppermute(value, "row", [(low, low - 1), (high, high + 1)])
        if hop == half - 2:
            return value, came
        value = jnp.where((place == low - 1) | (place == high + 1), came, value)


def per_device(children, block_maps):
    cols = lax.axis_size("col")
    rows = lax.axis_size("row")
    rows_dev, width = children.shape[1], children.shape[2]
    blocks_dev = width // PANEL
    part = rows_dev // cols
    both = 2 * PANEL

    spread = lax.all_to_all(pack(children, cols), "col", 0, 0, tiled=True)
    ordered = order(spread, block_maps)
    front = lax.all_to_all(ordered, "col", 0, 0, tiled=True)
    near, far = gather_col(ordered[0].reshape(2 * part, both), cols)
    panels, tile = gram_tile(near, far)
    state = gather_col(sum_row_small(tile, rows), cols)

    flat = front.reshape(cols * 2 * part, width)
    sums = []
    for b in range(blocks_dev):
        for p in range(2):
            left = panels[:, p * PANEL : (p + 1) * PANEL]
            right = flat[:, b * PANEL : (b + 1) * PANEL]
            sums.append(inwards(dot(left, right, ((0,), (0,))), rows))
    state, (one,) = stage(0, both, state, [sums[0]])
    one = across(one, rows)
    state, (two,) = stage(1, both, state, [sums[1]])
    two = across(two, rows)
    state, (three, one) = stage(2, both, state, [sums[2], one])
    one, three = outwards(one, rows), across(three, rows)
    state, (four, two) = stage(3, both, state, [sums[3], two])
    two, four = outwards(two, rows), across(four, rows)
    inv = state[1]
    basis = dot(panels, inv, ((1,), (1,)))
    three = outwards(three[0] + three[1], rows)
    four = outwards(four[0] + four[1], rows)
    outs = finish(0, inv, basis, front, (*one, *two), ())
    return finish(1, inv, basis, front, (*three, *four), outs)


def solution(mesh):
    placed = (P(None, "row", "col"), P())
    return jax.shard_map(
        per_device,
        mesh=mesh,
        in_specs=placed,
        out_specs=(P(None, "col"), P(None, "row", "col")),
        check_vma=False,
    )
```

```python
import jax
import jax.numpy as jnp
from jax import lax
from jax.experimental import pallas as pl
from jax.experimental.pallas import tpu as pltpu
from jax.sharding import PartitionSpec as P

PANEL = 256
LANES = 128
SUBS = 8
ANY = pl.BlockSpec(memory_space=pl.ANY)
VMEM = pl.BlockSpec(memory_space=pltpu.VMEM)
SMEM = pl.BlockSpec(memory_space=pltpu.SMEM)
KERNEL = pltpu.CompilerParams(vmem_limit_bytes=24 << 20)
F32 = jnp.float32


def dot(left, right, contract):
    return lax.dot_general(
        left,
        right,
        (contract, ((), ())),
        precision=lax.Precision.HIGHEST,
        preferred_element_type=F32,
    )


def shape(*dims):
    return jax.ShapeDtypeStruct(dims, F32)


def cost(flops, size):
    return pl.CostEstimate(flops=flops, bytes_accessed=size, transcendentals=0)


def run_copies(copies):
    for copy in copies:
        copy.start()
    for copy in copies:
        copy.wait()


def pack_kernel(children_ref, out_ref, sems):
    parts, _, part, _ = out_ref.shape
    run_copies(
        [
            pltpu.make_async_copy(
                children_ref.at[:, pl.ds(part * d, part), :], out_ref.at[d], sems.at[d]
            )
            for d in range(parts)
        ]
    )


def pack(children, parts):
    two, rows_dev, width = children.shape
    return pl.pallas_call(
        pack_kernel,
        out_shape=shape(parts, two, rows_dev // parts, width),
        in_specs=[ANY],
        out_specs=ANY,
        scratch_shapes=[pltpu.SemaphoreType.DMA((parts,))],
        compiler_params=KERNEL,
        cost_estimate=cost(0, 8 * children.size),
    )(children)


def order_kernel(maps_ref, spread_ref, out_ref, mine_ref, sems, mine_sems):
    owners, _, part, width = out_ref.shape
    per = width // PANEL
    copies = []
    for child in range(2):
        for block in range(owners * per):
            to = maps_ref[child, block]
            from_lane = (block % per) * PANEL
            to_lane = pl.multiple_of(lax.rem(to, per) * PANEL, PANEL)
            source = spread_ref.at[block // per, child, :, pl.ds(from_lane, PANEL)]
            copies.append(
                pltpu.make_async_copy(
                    source,
                    out_ref.at[lax.div(to, per), child, :, pl.ds(to_lane, PANEL)],
                    sems.at[child, block],
                )
            )

            @pl.when(to < 2)
            def _():
                pltpu.make_async_copy(
                    source,
                    mine_ref.at[pl.ds(child * part, part), pl.ds(to_lane, PANEL)],
                    mine_sems.at[child, to],
                ).start()

    run_copies(copies)
    for child in range(2):
        for panel in range(2):
            piece = mine_ref.at[pl.ds(child * part, part), pl.ds(panel * PANEL, PANEL)]
            pltpu.make_async_copy(piece, piece, mine_sems.at[child, panel]).wait()


def order(spread, maps):
    part, width = spread.shape[2:]
    return pl.pallas_call(
        order_kernel,
        out_shape=(shape(*spread.shape), shape(2 * part, 2 * PANEL)),
        in_specs=[SMEM, ANY],
        out_specs=(ANY, ANY),
        scratch_shapes=[
            pltpu.SemaphoreType.DMA(maps.shape),
            pltpu.SemaphoreType.DMA((2, 2)),
        ],
        compiler_params=KERNEL,
        cost_estimate=cost(0, 8 * spread.size),
        name="order",
    )(maps, spread)


def tile_kernel(near_ref, far_ref, panels_ref, tile_ref):
    me = lax.axis_index("col")
    half, part, both = near_ref.shape
    height = tile_ref.shape[0]
    groups = both // height
    for i in range(half):
        for ref, k in ((near_ref, 2 * i), (far_ref, 2 * i + 1)):
            at = pl.multiple_of(lax.bitwise_xor(me, k) * part, part)
            panels_ref[pl.ds(at, part), :] = ref[i]
    if height % LANES == 0:
        left = panels_ref[:, pl.ds(pl.multiple_of(lax.rem(me, groups) * height, height), height)]
    else:
        per = LANES // height
        group = lax.rem(me, groups)
        wide = panels_ref[:, pl.ds(pl.multiple_of(lax.div(group, per) * LANES, LANES), LANES)]
        left = wide[:, :height]
        for step in range(1, per):
            piece = wide[:, step * height : (step + 1) * height]
            left = jnp.where(lax.rem(group, per) == step, piece, left)
    right = panels_ref[:, pl.ds(pl.multiple_of(lax.div(me, groups) * LANES, LANES), LANES)]
    tile_ref[...] = dot(left, right, ((0,), (0,)))


def gram_tile(near, far):
    half, part, both = near.shape
    height = both * both // (2 * half * LANES)
    rows_dev = 2 * half * part
    return pl.pallas_call(
        tile_kernel,
        out_shape=(shape(rows_dev, both), shape(height, LANES)),
        in_specs=[VMEM, VMEM],
        out_specs=(VMEM, VMEM),
        compiler_params=KERNEL,
        cost_estimate=cost(12 * rows_dev * height * LANES, 12 * rows_dev * both),
    )(near, far)


def row_of(x, i):
    return jnp.broadcast_to(x[i : i + 1, :], (SUBS, LANES))


def column_of(x, j):
    return jnp.broadcast_to(x[:, j : j + 1], (SUBS, LANES))


def combined(weights, rows):
    p = [w * r for w, r in zip(weights, rows)]
    return ((p[0] + p[1]) + (p[2] + p[3])) + ((p[4] + p[5]) + (p[6] + p[7]))


def small_inverse(cols):
    sub = lax.broadcasted_iota(jnp.int32, (SUBS, LANES), 0)
    x = list(cols)
    t = [jnp.zeros((SUBS, LANES), F32) for _ in range(SUBS)]
    for j in range(SUBS):
        pivot = row_of(x[j], j)
        reciprocal = 1.0 / pivot
        root = lax.rsqrt(pivot)
        here = sub == j
        xj = x[j]
        for k in range(SUBS):
            if k == j:
                continue
            b = row_of(x[k], j)
            if k < j:
                t[k] = jnp.where(here, root * b, t[k])
            b = b * reciprocal
            x[k] = jnp.where(here, b, x[k] - xj * b)
        t[j] = jnp.where(here, root, t[j])
        x[j] = jnp.where(here, reciprocal, -xj * reciprocal)
    return x, t


def eliminate(index, a_ref, out_ref):
    size = a_ref.shape[0]
    lo = index // 2 * LANES
    hi = lo + LANES
    steps = LANES // SUBS
    first = index % 2 * (steps // 2)
    a = {i: a_ref[lo + SUBS * i : lo + SUBS * (i + 1), lo:hi] for i in range(first, steps)}
    e = {i: out_ref[lo + SUBS * i : lo + SUBS * (i + 1), lo:hi] for i in range(first, steps)}
    for s in range(first, first + steps // 2):
        inv, t = small_inverse([column_of(a[s], SUBS * s + k) for k in range(SUBS)])
        rows_a = [row_of(a[s], k) for k in range(SUBS)]
        rows_e = [row_of(e[s], k) for k in range(SUBS)]
        out_ref[lo + SUBS * s : lo + SUBS * (s + 1), lo:hi] = combined(t, rows_e)
        if s + 1 < steps:
            scaled_a, scaled_e = combined(inv, rows_a), combined(inv, rows_e)
            scaled_a = [row_of(scaled_a, k) for k in range(SUBS)]
            scaled_e = [row_of(scaled_e, k) for k in range(SUBS)]
            for i in range(s + 1, steps):
                c = [column_of(a[i], SUBS * s + k) for k in range(SUBS)]
                a[i] = a[i] - combined(c, scaled_a)
                e[i] = e[i] - combined(c, scaled_e)
    if first == 0:
        for i in range(steps // 2, steps):
            a_ref[lo + SUBS * i : lo + SUBS * (i + 1), lo:hi] = a[i]
            out_ref[lo + SUBS * i : lo + SUBS * (i + 1), lo:hi] = e[i]
        return
    inv = out_ref[lo:hi, lo:hi]
    if lo > 0:
        out_ref[lo:hi, :lo] = dot(inv, out_ref[lo:hi, :lo], ((1,), (0,)))
    if hi < size:
        right = dot(inv, a_ref[lo:hi, hi:], ((1,), (0,)))
        a_ref[hi:, hi:] = a_ref[hi:, hi:] - dot(right, right, ((0,), (0,)))
        out_ref[hi:, :hi] = out_ref[hi:, :hi] - dot(right, out_ref[lo:hi, :hi], ((0,), (0,)))


def stage_kernel(index, adds, extras, *refs):
    taken = refs[: 2 + 2 * adds]
    results = refs[2 + 2 * adds + extras :]
    a_ref, out_ref = results[:2]
    sums = results[2 : 2 + adds]
    landed, sems = results[2 + adds :]
    copies = [
        pltpu.make_async_copy(taken[3 + 2 * i], landed.at[i], sems.at[i]) for i in range(adds)
    ]
    for copy in copies:
        copy.start()
    if index == 0:
        me = lax.axis_index("col")
        near_ref, far_ref = taken[:2]
        half, height, _ = near_ref.shape
        size = a_ref.shape[0]
        groups = size // height
        for i in range(half):
            for ref, k in ((near_ref, 2 * i), (far_ref, 2 * i + 1)):
                at = lax.bitwise_xor(me, k)
                row = pl.multiple_of(lax.rem(at, groups) * height, height)
                lane = pl.multiple_of(lax.div(at, groups) * LANES, LANES)
                a_ref[pl.ds(row, height), pl.ds(lane, LANES)] = ref[i]
        down = lax.broadcasted_iota(jnp.int32, (size, size), 0)
        along = lax.broadcasted_iota(jnp.int32, (size, size), 1)
        out_ref[...] = jnp.where(down == along, 1.0, 0.0).astype(F32)
    eliminate(index, a_ref, out_ref)
    for i, copy in enumerate(copies):
        copy.wait()
        sums[i][...] = taken[2 + 2 * i][...] + landed[i]


def stage(index, size, state, adds=(), extras=()):
    flat = [ref for pair in adds for ref in pair]
    chunk = (PANEL, PANEL)
    outs = pl.pallas_call(
        lambda *refs: stage_kernel(index, len(adds), len(extras), *refs),
        out_shape=[shape(size, size)] * 2 + [shape(*chunk)] * len(adds),
        in_specs=[VMEM, VMEM] + [VMEM, ANY] * len(adds) + [ANY] * len(extras),
        out_specs=[VMEM] * (2 + len(adds)),
        input_output_aliases={0: 0, 1: 1} if index > 0 else {},
        scratch_shapes=[
            pltpu.VMEM((max(len(adds), 1),) + chunk, F32),
            pltpu.SemaphoreType.DMA((max(len(adds), 1),)),
        ],
        compiler_params=KERNEL,
        cost_estimate=cost(3_000_000_000, 4 * size * size),
        name="factor",
    )(*state, *flat, *extras)
    return outs[:2], outs[2:]


def finish_kernel(index, inv_ref, basis_ref, front_ref, *refs):
    given = 6 if index > 0 else 4
    chunks = refs[:4]
    upper_ref, trail_ref, m_ref, w_ref, f_ref, sems = refs[given:]
    rows = lax.axis_size("row")
    place = lax.axis_index("row")
    outer = (place == 0) | (place == rows - 1)
    for p in range(2):
        own, came = chunks[2 * p], chunks[2 * p + 1]
        into = m_ref.at[pl.ds(PANEL * p, PANEL), :]

        @pl.when(outer)
        def _():
            pltpu.make_async_copy(came, into, sems.at[p]).start()

        @pl.when(jnp.logical_not(outer))
        def _():
            pltpu.make_async_copy(own, into, sems.at[p]).start()

    for p in range(2):
        into = m_ref.at[pl.ds(PANEL * p, PANEL), :]
        pltpu.make_async_copy(chunks[2 * p], into, sems.at[p]).wait()
    w_ref[...] = dot(inv_ref[...], m_ref[...], ((1,), (0,)))
    columns = pl.ds(PANEL * index, PANEL)
    upper_copy = pltpu.make_async_copy(w_ref, upper_ref.at[:, columns], sems.at[0])
    upper_copy.start()
    product = dot(basis_ref[...], w_ref[...], ((1,), (0,)))
    owners, two, part = front_ref.shape[:3]
    for owner in range(owners):
        for child in range(two):
            at = (owner * two + child) * part
            f_ref[child, owner * part : (owner + 1) * part, :] = (
                front_ref[owner, child, :, PANEL * index : PANEL * (index + 1)]
                - product[at : at + part, :]
            )
    trail_copy = pltpu.make_async_copy(f_ref, trail_ref.at[:, :, columns], sems.at[1])
    trail_copy.start()
    upper_copy.wait()
    trail_copy.wait()


def finish(index, inv, basis, front, chunks, given):
    owners, two, part, width = front.shape
    both = inv.shape[0]
    outs = (shape(both, width), shape(two, owners * part, width))
    return pl.pallas_call(
        lambda *refs: finish_kernel(index, *refs),
        out_shape=outs,
        in_specs=[VMEM, VMEM, VMEM] + [ANY] * (4 + len(given)),
        out_specs=(ANY, ANY),
        input_output_aliases={7: 0, 8: 1} if given else {},
        scratch_shapes=[
            pltpu.VMEM((both, PANEL), F32),
            pltpu.VMEM((both, PANEL), F32),
            pltpu.VMEM((two, owners * part, PANEL), F32),
            pltpu.SemaphoreType.DMA((2,)),
        ],
        compiler_params=KERNEL,
        cost_estimate=cost(24 * both * both * PANEL, 24 * both * PANEL),
        name="finish",
    )(inv, basis, front, *chunks, *given)


def pairs_xor(size, mask):
    return [(i, i ^ mask) for i in range(size)]


def gather_col(piece, size):
    even = [piece] + [lax.ppermute(piece, "col", pairs_xor(size, k)) for k in range(2, size, 2)]
    near = jnp.stack(even)
    return near, lax.ppermute(near, "col", pairs_xor(size, 1))


def sum_row_small(value, size):
    span = 2
    while span <= size:
        value = value + lax.ppermute(value, "row", pairs_xor(size, span - 1))
        span *= 2
    return value


def inwards(value, size):
    for hop in range(size // 2 - 1):
        came = lax.ppermute(value, "row", [(hop, hop + 1), (size - 1 - hop, size - 2 - hop)])
        if hop == size // 2 - 2:
            return value, came
        value = value + came


def across(value, size):
    half = size // 2
    return value, lax.ppermute(value, "row", [(half - 1, half), (half, half - 1)])


def outwards(value, size):
    half = size // 2
    place = lax.axis_index("row")
    for hop in range(half - 1):
        low, high = half - 1 - hop, half + hop
        came = lax.ppermute(value, "row", [(low, low - 1), (high, high + 1)])
        if hop == half - 2:
            return value, came
        value = jnp.where((place == low - 1) | (place == high + 1), came, value)


def per_device(children, block_maps):
    cols = lax.axis_size("col")
    rows = lax.axis_size("row")
    rows_dev, width = children.shape[1], children.shape[2]
    blocks_dev = width // PANEL
    part = rows_dev // cols
    both = 2 * PANEL

    spread = lax.all_to_all(pack(children, cols), "col", 0, 0, tiled=True)
    ordered, mine = order(spread, block_maps)
    front = lax.all_to_all(ordered, "col", 0, 0, tiled=True)
    near, far = gather_col(mine, cols)
    panels, tile = gram_tile(near, far)
    state = gather_col(sum_row_small(tile, rows), cols)

    flat = front.reshape(cols * 2 * part, width)
    sums = []
    for b in range(blocks_dev):
        for p in range(2):
            left = panels[:, p * PANEL : (p + 1) * PANEL]
            right = flat[:, b * PANEL : (b + 1) * PANEL]
            sums.append(inwards(dot(left, right, ((0,), (0,))), rows))
    state, (one,) = stage(0, both, state, [sums[0]])
    one = across(one, rows)
    state, (two,) = stage(1, both, state, [sums[1]])
    two = across(two, rows)
    state, _ = stage(2, both, state)
    state, (three, one) = stage(3, both, state, [sums[2], one])
    one, three = outwards(one, rows), across(three, rows)
    state, (four, two) = stage(4, both, state, [sums[3], two])
    two, four = outwards(two, rows), across(four, rows)
    state, _ = stage(5, both, state)
    state, (three,) = stage(6, both, state, [three], [one[1]])
    three = outwards(three, rows)
    state, (four,) = stage(7, both, state, [four], [two[1]])
    four = outwards(four, rows)
    inv = state[1]
    basis = dot(panels, inv, ((1,), (1,)))
    outs = finish(0, inv, basis, front, (*one, *two), ())
    return finish(1, inv, basis, front, (*three, *four), outs)


def solution(mesh):
    placed = (P(None, "row", "col"), P())
    return jax.shard_map(
        per_device,
        mesh=mesh,
        in_specs=placed,
        out_specs=(P(None, "col"), P(None, "row", "col")),
        check_vma=False,
    )
```

```python
import jax
import jax.numpy as jnp
from jax import lax
from jax.experimental import pallas as pl
from jax.experimental.pallas import tpu as pltpu
from jax.sharding import PartitionSpec as P

PANEL = 256
LANES = 128
SUBS = 8
ANY = pl.BlockSpec(memory_space=pl.ANY)
VMEM = pl.BlockSpec(memory_space=pltpu.VMEM)
SMEM = pl.BlockSpec(memory_space=pltpu.SMEM)
KERNEL = pltpu.CompilerParams(vmem_limit_bytes=24 << 20)
F32 = jnp.float32


def dot(left, right, contract):
    return lax.dot_general(
        left,
        right,
        (contract, ((), ())),
        precision=lax.Precision.HIGHEST,
        preferred_element_type=F32,
    )


def shape(*dims):
    return jax.ShapeDtypeStruct(dims, F32)


def cost(flops, size):
    return pl.CostEstimate(flops=flops, bytes_accessed=size, transcendentals=0)


def run_copies(copies):
    for copy in copies:
        copy.start()
    for copy in copies:
        copy.wait()


def pack_kernel(children_ref, out_ref, sems):
    parts, _, part, _ = out_ref.shape
    run_copies(
        [
            pltpu.make_async_copy(
                children_ref.at[:, pl.ds(part * d, part), :], out_ref.at[d], sems.at[d]
            )
            for d in range(parts)
        ]
    )


def pack(children, parts):
    two, rows_dev, width = children.shape
    return pl.pallas_call(
        pack_kernel,
        out_shape=shape(parts, two, rows_dev // parts, width),
        in_specs=[ANY],
        out_specs=ANY,
        scratch_shapes=[pltpu.SemaphoreType.DMA((parts,))],
        compiler_params=KERNEL,
        cost_estimate=cost(1000, 1000),
    )(children)


def order_kernel(maps_ref, spread_ref, out_ref, mine_ref, sems, mine_sems):
    owners, _, part, width = out_ref.shape
    per = width // PANEL
    copies = []
    for child in range(2):
        for block in range(owners * per):
            to = maps_ref[child, block]
            from_lane = (block % per) * PANEL
            to_lane = pl.multiple_of(lax.rem(to, per) * PANEL, PANEL)
            source = spread_ref.at[block // per, child, :, pl.ds(from_lane, PANEL)]
            copies.append(
                pltpu.make_async_copy(
                    source,
                    out_ref.at[lax.div(to, per), child, :, pl.ds(to_lane, PANEL)],
                    sems.at[child, block],
                )
            )

            @pl.when(to < 2)
            def _():
                pltpu.make_async_copy(
                    source,
                    mine_ref.at[pl.ds(child * part, part), pl.ds(to_lane, PANEL)],
                    mine_sems.at[child, to],
                ).start()

    run_copies(copies)
    for child in range(2):
        for panel in range(2):
            piece = mine_ref.at[pl.ds(child * part, part), pl.ds(panel * PANEL, PANEL)]
            pltpu.make_async_copy(piece, piece, mine_sems.at[child, panel]).wait()


def order(spread, maps):
    part, width = spread.shape[2:]
    return pl.pallas_call(
        order_kernel,
        out_shape=(shape(*spread.shape), shape(2 * part, 2 * PANEL)),
        in_specs=[SMEM, ANY],
        out_specs=(ANY, ANY),
        scratch_shapes=[
            pltpu.SemaphoreType.DMA(maps.shape),
            pltpu.SemaphoreType.DMA((2, 2)),
        ],
        compiler_params=KERNEL,
        cost_estimate=cost(1000, 1000),
        name="order",
    )(maps, spread)


def tile_kernel(near_ref, far_ref, panels_ref, tile_ref):
    me = lax.axis_index("col")
    half, part, both = near_ref.shape
    height = tile_ref.shape[0]
    groups = both // height
    for i in range(half):
        for ref, k in ((near_ref, 2 * i), (far_ref, 2 * i + 1)):
            at = pl.multiple_of(lax.bitwise_xor(me, k) * part, part)
            panels_ref[pl.ds(at, part), :] = ref[i]
    if height % LANES == 0:
        left = panels_ref[:, pl.ds(pl.multiple_of(lax.rem(me, groups) * height, height), height)]
    else:
        per = LANES // height
        group = lax.rem(me, groups)
        wide = panels_ref[:, pl.ds(pl.multiple_of(lax.div(group, per) * LANES, LANES), LANES)]
        left = wide[:, :height]
        for step in range(1, per):
            piece = wide[:, step * height : (step + 1) * height]
            left = jnp.where(lax.rem(group, per) == step, piece, left)
    right = panels_ref[:, pl.ds(pl.multiple_of(lax.div(me, groups) * LANES, LANES), LANES)]
    tile_ref[...] = dot(left, right, ((0,), (0,)))


def gram_tile(near, far):
    half, part, both = near.shape
    height = both * both // (2 * half * LANES)
    rows_dev = 2 * half * part
    return pl.pallas_call(
        tile_kernel,
        out_shape=(shape(rows_dev, both), shape(height, LANES)),
        in_specs=[VMEM, VMEM],
        out_specs=(VMEM, VMEM),
        compiler_params=KERNEL,
        cost_estimate=cost(1000, 1000),
    )(near, far)


def row_of(x, i):
    return jnp.broadcast_to(x[i : i + 1, :], (SUBS, LANES))


def column_of(x, j):
    return jnp.broadcast_to(x[:, j : j + 1], (SUBS, LANES))


def combined(weights, rows):
    p = [w * r for w, r in zip(weights, rows)]
    return ((p[0] + p[1]) + (p[2] + p[3])) + ((p[4] + p[5]) + (p[6] + p[7]))


def small_inverse(cols):
    sub = lax.broadcasted_iota(jnp.int32, (SUBS, LANES), 0)
    x = list(cols)
    t = [jnp.zeros((SUBS, LANES), F32) for _ in range(SUBS)]
    for j in range(SUBS):
        pivot = row_of(x[j], j)
        reciprocal = 1.0 / pivot
        root = lax.rsqrt(pivot)
        here = sub == j
        xj = x[j]
        for k in range(SUBS):
            if k == j:
                continue
            b = row_of(x[k], j)
            if k < j:
                t[k] = jnp.where(here, root * b, t[k])
            b = b * reciprocal
            x[k] = jnp.where(here, b, x[k] - xj * b)
        t[j] = jnp.where(here, root, t[j])
        x[j] = jnp.where(here, reciprocal, -xj * reciprocal)
    return x, t


def factor_inverse(lo, a_ref, out_ref):
    hi = lo + LANES
    steps = LANES // SUBS
    lane = lax.broadcasted_iota(jnp.int32, (SUBS, LANES), 1)
    sub = lax.broadcasted_iota(jnp.int32, (SUBS, LANES), 0)
    z = [a_ref[lo + SUBS * i : lo + SUBS * (i + 1), lo:hi] for i in range(steps)]
    for s in range(steps):
        inv, t = small_inverse([column_of(z[s], SUBS * s + k) for k in range(SUBS)])
        here = (lane >= SUBS * s) & (lane < SUBS * (s + 1))
        own = jnp.where(here, jnp.where(lane == sub + SUBS * s, 1.0, 0.0), z[s])
        rows = [row_of(own, k) for k in range(SUBS)]
        out_ref[lo + SUBS * s : lo + SUBS * (s + 1), lo:hi] = jnp.where(
            lane < SUBS * (s + 1), combined(t, rows), 0.0
        )
        if s + 1 < steps:
            scaled = combined(inv, rows)
            scaled = [row_of(scaled, k) for k in range(SUBS)]
            for i in range(s + 1, steps):
                c = [column_of(z[i], SUBS * s + k) for k in range(SUBS)]
                z[i] = jnp.where(here, 0.0, z[i]) - combined(c, scaled)


def stage_kernel(lo, *refs):
    a_ref, out_ref = refs[-2:]
    size, hi = a_ref.shape[0], lo + LANES
    if lo == 0:
        me = lax.axis_index("col")
        near_ref, far_ref = refs[:2]
        half, height, _ = near_ref.shape
        groups = size // height
        for i in range(half):
            for ref, k in ((near_ref, 2 * i), (far_ref, 2 * i + 1)):
                at = lax.bitwise_xor(me, k)
                row = pl.multiple_of(lax.rem(at, groups) * height, height)
                lane = pl.multiple_of(lax.div(at, groups) * LANES, LANES)
                a_ref[pl.ds(row, height), pl.ds(lane, LANES)] = ref[i]
        out_ref[...] = jnp.zeros_like(out_ref)
    factor_inverse(lo, a_ref, out_ref)
    inv = out_ref[lo:hi, lo:hi]
    if lo > 0:
        out_ref[lo:hi, :lo] = dot(inv, out_ref[lo:hi, :lo], ((1,), (0,)))
    if hi < size:
        right = dot(inv, a_ref[lo:hi, hi:], ((1,), (0,)))
        a_ref[hi:, hi:] = a_ref[hi:, hi:] - dot(right, right, ((0,), (0,)))
        out_ref[hi:, :hi] = out_ref[hi:, :hi] - dot(right, out_ref[lo:hi, :hi], ((0,), (0,)))


def stage(lo, state, after=()):
    size = 2 * PANEL
    return pl.pallas_call(
        lambda *refs: stage_kernel(lo, *refs),
        out_shape=(shape(size, size), shape(size, size)),
        in_specs=[VMEM, VMEM] + [ANY] * len(after),
        out_specs=(VMEM, VMEM),
        input_output_aliases={0: 0, 1: 1} if lo > 0 else {},
        compiler_params=KERNEL,
        cost_estimate=cost(1000, 1000),
        name="stage",
    )(*state, *after)


def stack_kernel(count, *refs):
    for i in range(count):
        refs[-1][i] = refs[i][...]


def stack_after(pieces, after):
    return pl.pallas_call(
        lambda *refs: stack_kernel(len(pieces), *refs),
        out_shape=shape(len(pieces), *pieces[0].shape),
        in_specs=[VMEM] * len(pieces) + [ANY] * len(after),
        out_specs=VMEM,
        compiler_params=KERNEL,
        cost_estimate=cost(1000, 1000),
        name="stack",
    )(*pieces, *after)


def multiply_kernel(panels_ref, front_ref, *refs):
    out_ref, held_ref, sems = refs[-3:]
    count, _, width = out_ref.shape
    step = max(width, PANEL)
    copies = []
    for lane in range(0, count * width, step):
        product = dot(panels_ref[...], front_ref[:, lane : lane + step], ((0,), (0,)))
        for at in range(0, step, width):
            n = (lane + at) // width
            held_ref[n] = product[:, at : at + width]
            copies.append(pltpu.make_async_copy(held_ref.at[n], out_ref.at[n], sems.at[n]))
            copies[-1].start()
    for copy in copies:
        copy.wait()


def multiply(panels, front, count, after):
    both = panels.shape[1]
    part = (count, both, front.shape[1] // count)
    return pl.pallas_call(
        multiply_kernel,
        out_shape=shape(*part),
        in_specs=[VMEM, VMEM] + [ANY] * len(after),
        out_specs=ANY,
        scratch_shapes=[pltpu.VMEM(part, F32), pltpu.SemaphoreType.DMA((count,))],
        compiler_params=KERNEL,
        cost_estimate=cost(1000, 1000),
        name="multiply",
    )(panels, front, *after)


def hold(array, after):
    return pl.pallas_call(
        lambda *refs: None,
        out_shape=shape(*array.shape),
        in_specs=[ANY] * (1 + len(after)),
        out_specs=ANY,
        input_output_aliases={0: 0},
        compiler_params=KERNEL,
        cost_estimate=cost(1000, 1000),
        name="hold",
    )(array, *after)


def total_kernel(parts_ref, out_ref):
    total = parts_ref[0]
    for i in range(1, parts_ref.shape[0]):
        total = total + parts_ref[i]
    out_ref[...] = total


def total_of(parts):
    return pl.pallas_call(
        total_kernel,
        out_shape=shape(*parts.shape[1:]),
        in_specs=[VMEM],
        out_specs=VMEM,
        compiler_params=KERNEL,
        cost_estimate=cost(1000, 1000),
        name="total",
    )(parts)


def finish_kernel(masks, inv_ref, basis_ref, front_ref, *refs):
    upper_ref, trail_ref, m_ref, w_ref, f_ref, sems = refs[-6:]
    owners, two, part, total = front_ref.shape
    width = refs[0].shape[1]
    for n in range(len(masks)):
        m_ref[:, n * width : (n + 1) * width] = refs[n][...]
    w_ref[...] = dot(inv_ref[...], m_ref[...], ((1,), (0,)))
    copies = []
    columns = []
    for n, mask in enumerate(masks):
        if width == total:
            columns.append(pl.ds(0, width))
        else:
            at = lax.bitwise_xor(lax.axis_index("row"), mask) * width
            columns.append(pl.ds(pl.multiple_of(at, LANES), width))
        held = w_ref.at[:, pl.ds(n * width, width)]
        copies.append(pltpu.make_async_copy(held, upper_ref.at[:, columns[n]], sems.at[0, n]))
        copies[-1].start()
    product = dot(basis_ref[...], w_ref[...], ((1,), (0,)))
    for n, mask in enumerate(masks):
        for owner in range(owners):
            for child in range(two):
                row = (owner * two + child) * part
                f_ref[n, child, owner * part : (owner + 1) * part, :] = (
                    front_ref[owner, child, :, columns[n]]
                    - product[row : row + part, n * width : (n + 1) * width]
                )
        copies.append(
            pltpu.make_async_copy(f_ref.at[n], trail_ref.at[:, :, columns[n]], sems.at[1, n])
        )
        copies[-1].start()
    for copy in copies:
        copy.wait()


def finish(pieces, inv, basis, front, given):
    owners, two, part, total = front.shape
    masks = [mask for mask, _ in pieces]
    arrays = [array for _, array in pieces]
    count = len(pieces)
    both, width = arrays[0].shape
    return pl.pallas_call(
        lambda *refs: finish_kernel(masks, *refs),
        out_shape=(shape(both, total), shape(two, owners * part, total)),
        in_specs=[VMEM] * (3 + count) + [ANY] * len(given),
        out_specs=(ANY, ANY),
        input_output_aliases={3 + count: 0, 4 + count: 1} if given else {},
        scratch_shapes=[
            pltpu.VMEM((both, count * width), F32),
            pltpu.VMEM((both, count * width), F32),
            pltpu.VMEM((count, two, owners * part, width), F32),
            pltpu.SemaphoreType.DMA((2, count)),
        ],
        compiler_params=KERNEL,
        cost_estimate=cost(1000, 1000),
        name="finish",
    )(inv, basis, front, *arrays, *given)


def pairs_xor(size, mask):
    return [(i, i ^ mask) for i in range(size)]


def even_pieces(piece, size):
    return [piece] + [lax.ppermute(piece, "col", pairs_xor(size, k)) for k in range(2, size, 2)]


def gather_col(piece, size):
    near = jnp.stack(even_pieces(piece, size))
    return near, lax.ppermute(near, "col", pairs_xor(size, 1))


def sum_row_small(value, size):
    span = 2
    while span <= size:
        value = value + lax.ppermute(value, "row", pairs_xor(size, span - 1))
        span *= 2
    return value


def per_device(children, block_maps):
    cols = lax.axis_size("col")
    rows = lax.axis_size("row")
    rows_dev, width = children.shape[1], children.shape[2]
    blocks_dev = width // PANEL
    part = rows_dev // cols
    both = 2 * PANEL

    spread = lax.all_to_all(pack(children, cols), "col", 0, 0, tiled=True)
    ordered, mine = order(spread, block_maps)
    pieces = even_pieces(mine, cols)
    front = lax.all_to_all(hold(ordered, pieces[1:2]), "col", 0, 0, tiled=True)
    near = stack_after(pieces, [])
    panels, tile = gram_tile(near, lax.ppermute(near, "col", pairs_xor(cols, 1)))
    tile = sum_row_small(tile, rows)
    tiles = even_pieces(tile, cols)

    flat = front.reshape(cols * 2 * part, width)
    products = multiply(panels, flat, rows, [tile])
    parts = lax.all_to_all(products, "row", 0, 0, tiled=True)
    near = stack_after(tiles, [products])
    state = near, lax.ppermute(near, "col", pairs_xor(cols, 1))
    for lo in range(0, both - LANES, LANES):
        state = stage(lo, state)
    mine = total_of(parts)
    _, inv = stage(both - LANES, state, [mine])
    basis = dot(panels, inv, ((1,), (1,)))
    masks = sorted(range(1, rows), key=lambda k: (k.bit_length(), -k))
    pieces = [(0, mine)]
    pieces += [(k, lax.ppermute(mine, "row", pairs_xor(rows, k))) for k in masks]
    if mine.shape[1] % LANES:
        place = lax.axis_index("row")
        ordered = jnp.stack([piece for _, piece in sorted(pieces, key=lambda p: p[0])])
        ordered = jnp.take(ordered, jnp.arange(rows, dtype=jnp.int32) ^ place, axis=0)
        pieces = [(0, ordered.transpose(1, 0, 2).reshape(both, width))]
    outs = ()
    for n in range(0, len(pieces), 2):
        outs = finish(pieces[n : n + 2], inv, basis, front, outs)
    return outs


def solution(mesh):
    placed = (P(None, "row", "col"), P())
    return jax.shard_map(
        per_device,
        mesh=mesh,
        in_specs=placed,
        out_specs=(P(None, "col"), P(None, "row", "col")),
        check_vma=False,
    )
```

```python
import jax
import jax.numpy as jnp
from jax import lax
from jax.experimental import pallas as pl
from jax.experimental.pallas import tpu as pltpu
from jax.sharding import PartitionSpec as P

PANEL = 256
LANES = 128
SUBS = 8
ANY = pl.BlockSpec(memory_space=pl.ANY)
VMEM = pl.BlockSpec(memory_space=pltpu.VMEM)
SMEM = pl.BlockSpec(memory_space=pltpu.SMEM)
KERNEL = pltpu.CompilerParams(vmem_limit_bytes=24 << 20)
F32 = jnp.float32


def dot(left, right, contract):
    return lax.dot_general(
        left,
        right,
        (contract, ((), ())),
        precision=lax.Precision.HIGHEST,
        preferred_element_type=F32,
    )


def shape(*dims):
    return jax.ShapeDtypeStruct(dims, F32)


def cost(flops, size):
    return pl.CostEstimate(flops=flops, bytes_accessed=size, transcendentals=0)


def run_copies(copies):
    for copy in copies:
        copy.start()
    for copy in copies:
        copy.wait()


def pack_kernel(children_ref, out_ref, sems):
    parts, _, part, _ = out_ref.shape
    run_copies(
        [
            pltpu.make_async_copy(
                children_ref.at[:, pl.ds(part * d, part), :], out_ref.at[d], sems.at[d]
            )
            for d in range(parts)
        ]
    )


def pack(children, parts):
    two, rows_dev, width = children.shape
    return pl.pallas_call(
        pack_kernel,
        out_shape=shape(parts, two, rows_dev // parts, width),
        in_specs=[ANY],
        out_specs=ANY,
        scratch_shapes=[pltpu.SemaphoreType.DMA((parts,))],
        compiler_params=KERNEL,
        cost_estimate=cost(1000, 1000),
    )(children)


def order_kernel(maps_ref, spread_ref, out_ref, mine_ref, sems, mine_sems):
    owners, _, part, width = out_ref.shape
    per = width // PANEL
    copies = []
    for child in range(2):
        for block in range(owners * per):
            to = maps_ref[child, block]
            from_lane = (block % per) * PANEL
            to_lane = pl.multiple_of(lax.rem(to, per) * PANEL, PANEL)
            source = spread_ref.at[block // per, child, :, pl.ds(from_lane, PANEL)]
            copies.append(
                pltpu.make_async_copy(
                    source,
                    out_ref.at[lax.div(to, per), child, :, pl.ds(to_lane, PANEL)],
                    sems.at[child, block],
                )
            )

            @pl.when(to < 2)
            def _():
                pltpu.make_async_copy(
                    source,
                    mine_ref.at[pl.ds(child * part, part), pl.ds(to_lane, PANEL)],
                    mine_sems.at[child, to],
                ).start()

    run_copies(copies)
    for child in range(2):
        for panel in range(2):
            piece = mine_ref.at[pl.ds(child * part, part), pl.ds(panel * PANEL, PANEL)]
            pltpu.make_async_copy(piece, piece, mine_sems.at[child, panel]).wait()


def order(spread, maps):
    part, width = spread.shape[2:]
    return pl.pallas_call(
        order_kernel,
        out_shape=(shape(*spread.shape), shape(2 * part, 2 * PANEL)),
        in_specs=[SMEM, ANY],
        out_specs=(ANY, ANY),
        scratch_shapes=[
            pltpu.SemaphoreType.DMA(maps.shape),
            pltpu.SemaphoreType.DMA((2, 2)),
        ],
        compiler_params=KERNEL,
        cost_estimate=cost(1000, 1000),
        name="order",
    )(maps, spread)


def tile_kernel(near_ref, far_ref, panels_ref, tile_ref):
    me = lax.axis_index("col")
    half, part, both = near_ref.shape
    height = tile_ref.shape[0]
    groups = both // height
    for i in range(half):
        for ref, k in ((near_ref, 2 * i), (far_ref, 2 * i + 1)):
            at = pl.multiple_of(lax.bitwise_xor(me, k) * part, part)
            panels_ref[pl.ds(at, part), :] = ref[i]
    if height % LANES == 0:
        left = panels_ref[:, pl.ds(pl.multiple_of(lax.rem(me, groups) * height, height), height)]
    else:
        per = LANES // height
        group = lax.rem(me, groups)
        wide = panels_ref[:, pl.ds(pl.multiple_of(lax.div(group, per) * LANES, LANES), LANES)]
        left = wide[:, :height]
        for step in range(1, per):
            piece = wide[:, step * height : (step + 1) * height]
            left = jnp.where(lax.rem(group, per) == step, piece, left)
    right = panels_ref[:, pl.ds(pl.multiple_of(lax.div(me, groups) * LANES, LANES), LANES)]
    tile_ref[...] = dot(left, right, ((0,), (0,)))


def gram_tile(near, far):
    half, part, both = near.shape
    height = both * both // (2 * half * LANES)
    rows_dev = 2 * half * part
    return pl.pallas_call(
        tile_kernel,
        out_shape=(shape(rows_dev, both), shape(height, LANES)),
        in_specs=[VMEM, VMEM],
        out_specs=(VMEM, VMEM),
        compiler_params=KERNEL,
        cost_estimate=cost(1000, 1000),
    )(near, far)


def row_of(x, i):
    return jnp.broadcast_to(x[i : i + 1, :], (SUBS, LANES))


def column_of(x, j):
    return jnp.broadcast_to(x[:, j : j + 1], (SUBS, LANES))


def combined(weights, rows):
    p = [w * r for w, r in zip(weights, rows)]
    return ((p[0] + p[1]) + (p[2] + p[3])) + ((p[4] + p[5]) + (p[6] + p[7]))


def factor_inverse(lo, a_ref, out_ref):
    hi = lo + LANES
    steps = LANES // SUBS
    lane = lax.broadcasted_iota(jnp.int32, (SUBS, LANES), 1)
    sub = lax.broadcasted_iota(jnp.int32, (SUBS, LANES), 0)
    z = [a_ref[lo + SUBS * i : lo + SUBS * (i + 1), lo:hi] for i in range(steps)]
    for s in range(steps):
        x = [column_of(z[s], SUBS * s + k) for k in range(SUBS)]
        block = (lane >= SUBS * s) & (lane < SUBS * (s + 1))
        slab = jnp.where(block, jnp.where(lane == sub + SUBS * s, 1.0, 0.0), z[s])
        out = jnp.zeros((SUBS, LANES), F32)
        for j in range(SUBS):
            here = sub == j
            pivot = row_of(x[j], j)
            reciprocal = 1.0 / pivot
            for k in range(j + 1, SUBS):
                b = row_of(x[k], j) * reciprocal
                x[k] = jnp.where(here, b, x[k] - x[j] * b)
            row = row_of(slab, j)
            out = jnp.where(here, lax.rsqrt(pivot) * row, out)
            row = row * reciprocal
            slab = jnp.where(here, row, slab - x[j] * row)
        out_ref[lo + SUBS * s : lo + SUBS * (s + 1), lo:hi] = jnp.where(
            lane < SUBS * (s + 1), out, 0.0
        )
        if s + 1 < steps:
            c = [column_of(z[s + 1], SUBS * s + k) for k in range(SUBS)]
            change = combined(c, [row_of(slab, k) for k in range(SUBS)])
            z[s + 1] = jnp.where(block, 0.0, z[s + 1]) - change
        if s + 2 < steps:
            below = jnp.concatenate(z[s + 2 :], axis=0)
            around = [jnp.zeros((SUBS, LANES), F32)] * steps
            around[s] = slab
            change = dot(below, jnp.concatenate(around, axis=0), ((1,), (0,)))
            for i in range(s + 2, steps):
                at = SUBS * (i - s - 2)
                z[i] = jnp.where(block, 0.0, z[i]) - change[at : at + SUBS, :]


def stage_kernel(lo, *refs):
    a_ref, out_ref = refs[-2:]
    size, hi = a_ref.shape[0], lo + LANES
    if lo == 0:
        me = lax.axis_index("col")
        near_ref, far_ref = refs[:2]
        half, height, _ = near_ref.shape
        groups = size // height
        for i in range(half):
            for ref, k in ((near_ref, 2 * i), (far_ref, 2 * i + 1)):
                at = lax.bitwise_xor(me, k)
                row = pl.multiple_of(lax.rem(at, groups) * height, height)
                lane = pl.multiple_of(lax.div(at, groups) * LANES, LANES)
                a_ref[pl.ds(row, height), pl.ds(lane, LANES)] = ref[i]
        out_ref[...] = jnp.zeros_like(out_ref)
    factor_inverse(lo, a_ref, out_ref)
    inv = out_ref[lo:hi, lo:hi]
    if lo > 0:
        out_ref[lo:hi, :lo] = dot(inv, out_ref[lo:hi, :lo], ((1,), (0,)))
    if hi < size:
        right = dot(inv, a_ref[lo:hi, hi:], ((1,), (0,)))
        a_ref[hi:, hi:] = a_ref[hi:, hi:] - dot(right, right, ((0,), (0,)))
        out_ref[hi:, :hi] = out_ref[hi:, :hi] - dot(right, out_ref[lo:hi, :hi], ((0,), (0,)))


def stage(lo, state, after=()):
    size = 2 * PANEL
    return pl.pallas_call(
        lambda *refs: stage_kernel(lo, *refs),
        out_shape=(shape(size, size), shape(size, size)),
        in_specs=[VMEM, VMEM] + [ANY] * len(after),
        out_specs=(VMEM, VMEM),
        input_output_aliases={0: 0, 1: 1} if lo > 0 else {},
        compiler_params=KERNEL,
        cost_estimate=cost(1000, 1000),
        name="stage",
    )(*state, *after)


def stack_kernel(count, *refs):
    for i in range(count):
        refs[-1][i] = refs[i][...]


def stack_after(pieces, after):
    return pl.pallas_call(
        lambda *refs: stack_kernel(len(pieces), *refs),
        out_shape=shape(len(pieces), *pieces[0].shape),
        in_specs=[VMEM] * len(pieces) + [ANY] * len(after),
        out_specs=VMEM,
        compiler_params=KERNEL,
        cost_estimate=cost(1000, 1000),
        name="stack",
    )(*pieces, *after)


def multiply_kernel(panels_ref, front_ref, *refs):
    out_ref, held_ref, sems = refs[-3:]
    count, _, width = out_ref.shape
    step = max(width, PANEL)
    copies = []
    for lane in range(0, count * width, step):
        product = dot(panels_ref[...], front_ref[:, lane : lane + step], ((0,), (0,)))
        for at in range(0, step, width):
            n = (lane + at) // width
            held_ref[n] = product[:, at : at + width]
            copies.append(pltpu.make_async_copy(held_ref.at[n], out_ref.at[n], sems.at[n]))
            copies[-1].start()
    for copy in copies:
        copy.wait()


def multiply(panels, front, count, after):
    both = panels.shape[1]
    part = (count, both, front.shape[1] // count)
    return pl.pallas_call(
        multiply_kernel,
        out_shape=shape(*part),
        in_specs=[VMEM, VMEM] + [ANY] * len(after),
        out_specs=ANY,
        scratch_shapes=[pltpu.VMEM(part, F32), pltpu.SemaphoreType.DMA((count,))],
        compiler_params=KERNEL,
        cost_estimate=cost(1000, 1000),
        name="multiply",
    )(panels, front, *after)


def hold(array, after):
    return pl.pallas_call(
        lambda *refs: None,
        out_shape=shape(*array.shape),
        in_specs=[ANY] * (1 + len(after)),
        out_specs=ANY,
        input_output_aliases={0: 0},
        compiler_params=KERNEL,
        cost_estimate=cost(1000, 1000),
        name="hold",
    )(array, *after)


def total_kernel(parts_ref, out_ref):
    total = parts_ref[0]
    for i in range(1, parts_ref.shape[0]):
        total = total + parts_ref[i]
    out_ref[...] = total


def total_of(parts):
    return pl.pallas_call(
        total_kernel,
        out_shape=shape(*parts.shape[1:]),
        in_specs=[VMEM],
        out_specs=VMEM,
        compiler_params=KERNEL,
        cost_estimate=cost(1000, 1000),
        name="total",
    )(parts)


def finish_kernel(masks, inv_ref, basis_ref, front_ref, *refs):
    upper_ref, trail_ref, m_ref, w_ref, f_ref, sems = refs[-6:]
    owners, two, part, total = front_ref.shape
    both = inv_ref.shape[0]
    width = refs[0].shape[1]
    columns = []
    for n, mask in enumerate(masks):
        m_ref[:, n * width : (n + 1) * width] = refs[n][...]
        if width == total:
            columns.append(pl.ds(0, width))
        else:
            at = lax.bitwise_xor(lax.axis_index("row"), mask) * width
            columns.append(pl.ds(pl.multiple_of(at, LANES), width))
    copies = []
    for step in range(both // LANES):
        lo, hi = step * LANES, (step + 1) * LANES
        w_ref[lo:hi, :] = dot(inv_ref[lo:hi, :hi], m_ref[:hi, :], ((1,), (0,)))
        for n in range(len(masks)):
            held = w_ref.at[lo:hi, pl.ds(n * width, width)]
            goal = upper_ref.at[lo:hi, columns[n]]
            copies.append(pltpu.make_async_copy(held, goal, sems.at[0, n, step]))
            copies[-1].start()
    rows = LANES // two
    held_owners = rows // part
    for step in range(owners // held_owners):
        lo = step * LANES
        product = dot(basis_ref[lo : lo + LANES, :], w_ref[...], ((1,), (0,)))
        for n in range(len(masks)):
            for owner in range(held_owners):
                for child in range(two):
                    row = (owner * two + child) * part
                    at = step * rows + owner * part
                    f_ref[n, child, at : at + part, :] = (
                        front_ref[step * held_owners + owner, child, :, columns[n]]
                        - product[row : row + part, n * width : (n + 1) * width]
                    )
            held = f_ref.at[n, :, pl.ds(step * rows, rows), :]
            goal = trail_ref.at[:, pl.ds(step * rows, rows), columns[n]]
            copies.append(pltpu.make_async_copy(held, goal, sems.at[1, n, step]))
            copies[-1].start()
    for copy in copies:
        copy.wait()


def finish(pieces, inv, basis, front, given):
    owners, two, part, total = front.shape
    masks = [mask for mask, _ in pieces]
    arrays = [array for _, array in pieces]
    count = len(pieces)
    both, width = arrays[0].shape
    return pl.pallas_call(
        lambda *refs: finish_kernel(masks, *refs),
        out_shape=(shape(both, total), shape(two, owners * part, total)),
        in_specs=[VMEM] * (3 + count) + [ANY] * len(given),
        out_specs=(ANY, ANY),
        input_output_aliases={3 + count: 0, 4 + count: 1} if given else {},
        scratch_shapes=[
            pltpu.VMEM((both, count * width), F32),
            pltpu.VMEM((both, count * width), F32),
            pltpu.VMEM((count, two, owners * part, width), F32),
            pltpu.SemaphoreType.DMA((2, count, both // LANES)),
        ],
        compiler_params=KERNEL,
        cost_estimate=cost(1000, 1000),
        name="finish",
    )(inv, basis, front, *arrays, *given)


def pairs_xor(size, mask):
    return [(i, i ^ mask) for i in range(size)]


def even_pieces(piece, size):
    return [piece] + [lax.ppermute(piece, "col", pairs_xor(size, k)) for k in range(2, size, 2)]


def gather_col(piece, size):
    near = jnp.stack(even_pieces(piece, size))
    return near, lax.ppermute(near, "col", pairs_xor(size, 1))


def sum_row_small(value, size):
    span = 2
    while span <= size:
        value = value + lax.ppermute(value, "row", pairs_xor(size, span - 1))
        span *= 2
    return value


def per_device(children, block_maps):
    cols = lax.axis_size("col")
    rows = lax.axis_size("row")
    rows_dev, width = children.shape[1], children.shape[2]
    blocks_dev = width // PANEL
    part = rows_dev // cols
    both = 2 * PANEL

    spread = lax.all_to_all(pack(children, cols), "col", 0, 0, tiled=True)
    ordered, mine = order(spread, block_maps)
    pieces = even_pieces(mine, cols)
    front = lax.all_to_all(hold(ordered, pieces[1:2]), "col", 0, 0, tiled=True)
    near = stack_after(pieces, [])
    panels, tile = gram_tile(near, lax.ppermute(near, "col", pairs_xor(cols, 1)))
    tile = sum_row_small(tile, rows)
    tiles = even_pieces(tile, cols)

    flat = front.reshape(cols * 2 * part, width)
    products = multiply(panels, flat, rows, [tile])
    parts = lax.all_to_all(products, "row", 0, 0, tiled=True)
    near = stack_after(tiles, [products])
    state = near, lax.ppermute(near, "col", pairs_xor(cols, 1))
    for lo in range(0, both - LANES, LANES):
        state = stage(lo, state)
    mine = total_of(parts)
    _, inv = stage(both - LANES, state, [mine])
    basis = dot(panels, inv, ((1,), (1,)))
    masks = sorted(range(1, rows), key=lambda k: (k.bit_length(), -k))
    pieces = [(0, mine)]
    pieces += [(k, lax.ppermute(mine, "row", pairs_xor(rows, k))) for k in masks]
    if mine.shape[1] % LANES:
        place = lax.axis_index("row")
        ordered = jnp.stack([piece for _, piece in sorted(pieces, key=lambda p: p[0])])
        ordered = jnp.take(ordered, jnp.arange(rows, dtype=jnp.int32) ^ place, axis=0)
        pieces = [(0, ordered.transpose(1, 0, 2).reshape(both, width))]
    outs = ()
    for n in range(0, len(pieces), 2):
        outs = finish(pieces[n : n + 2], inv, basis, front, outs)
    return outs


def solution(mesh):
    placed = (P(None, "row", "col"), P())
    return jax.shard_map(
        per_device,
        mesh=mesh,
        in_specs=placed,
        out_specs=(P(None, "col"), P(None, "row", "col")),
        check_vma=False,
    )
```

```python
import jax
import jax.numpy as jnp
from jax import lax
from jax.experimental import pallas as pl
from jax.experimental.pallas import tpu as pltpu
from jax.sharding import PartitionSpec as P

PANEL = 256
LANES = 128
SUBS = 8
ANY = pl.BlockSpec(memory_space=pl.ANY)
VMEM = pl.BlockSpec(memory_space=pltpu.VMEM)
SMEM = pl.BlockSpec(memory_space=pltpu.SMEM)
KERNEL = pltpu.CompilerParams(vmem_limit_bytes=24 << 20)
F32 = jnp.float32


def dot(left, right, contract):
    return lax.dot_general(
        left,
        right,
        (contract, ((), ())),
        precision=lax.Precision.HIGHEST,
        preferred_element_type=F32,
    )


def shape(*dims):
    return jax.ShapeDtypeStruct(dims, F32)


def cost(flops, size):
    return pl.CostEstimate(flops=flops, bytes_accessed=size, transcendentals=0)


def run_copies(copies):
    for copy in copies:
        copy.start()
    for copy in copies:
        copy.wait()


def pack_kernel(children_ref, out_ref, sems):
    parts, _, part, _ = out_ref.shape
    run_copies(
        [
            pltpu.make_async_copy(
                children_ref.at[:, pl.ds(part * d, part), :], out_ref.at[d], sems.at[d]
            )
            for d in range(parts)
        ]
    )


def pack(children, parts):
    two, rows_dev, width = children.shape
    return pl.pallas_call(
        pack_kernel,
        out_shape=shape(parts, two, rows_dev // parts, width),
        in_specs=[ANY],
        out_specs=ANY,
        scratch_shapes=[pltpu.SemaphoreType.DMA((parts,))],
        compiler_params=KERNEL,
        cost_estimate=cost(1000, 1000),
    )(children)


def order_kernel(maps_ref, spread_ref, out_ref, mine_ref, sems, mine_sems):
    owners, _, part, width = out_ref.shape
    per = width // PANEL
    copies = []
    for child in range(2):
        for block in range(owners * per):
            to = maps_ref[child, block]
            from_lane = (block % per) * PANEL
            to_lane = pl.multiple_of(lax.rem(to, per) * PANEL, PANEL)
            source = spread_ref.at[block // per, child, :, pl.ds(from_lane, PANEL)]
            copies.append(
                pltpu.make_async_copy(
                    source,
                    out_ref.at[lax.div(to, per), child, :, pl.ds(to_lane, PANEL)],
                    sems.at[child, block],
                )
            )

            @pl.when(to < 2)
            def _():
                pltpu.make_async_copy(
                    source,
                    mine_ref.at[pl.ds(child * part, part), pl.ds(to_lane, PANEL)],
                    mine_sems.at[child, to],
                ).start()

    run_copies(copies)
    for child in range(2):
        for panel in range(2):
            piece = mine_ref.at[pl.ds(child * part, part), pl.ds(panel * PANEL, PANEL)]
            pltpu.make_async_copy(piece, piece, mine_sems.at[child, panel]).wait()


def order(spread, maps):
    part, width = spread.shape[2:]
    return pl.pallas_call(
        order_kernel,
        out_shape=(shape(*spread.shape), shape(2 * part, 2 * PANEL)),
        in_specs=[SMEM, ANY],
        out_specs=(ANY, ANY),
        scratch_shapes=[
            pltpu.SemaphoreType.DMA(maps.shape),
            pltpu.SemaphoreType.DMA((2, 2)),
        ],
        compiler_params=KERNEL,
        cost_estimate=cost(1000, 1000),
        name="order",
    )(maps, spread)


def lower_blocks(size):
    return [(i, j) for i in range(size // LANES) for j in range(i + 1)]


def tile_kernel(near_ref, far_ref, panels_ref, tile_ref, blocks_ref):
    me = lax.axis_index("col")
    half, part, both = near_ref.shape
    height = tile_ref.shape[0]
    for i in range(half):
        for ref, k in ((near_ref, 2 * i), (far_ref, 2 * i + 1)):
            at = pl.multiple_of(lax.bitwise_xor(me, k) * part, part)
            panels_ref[pl.ds(at, part), :] = ref[i]
    last = len(lower_blocks(both)) - 1
    start = me * height
    first = lax.div(start, LANES)
    for n in range(2):
        block = lax.min(first + n, last)
        row = jnp.int32(0)
        for i in range(1, both // LANES):
            row = row + (block >= i * (i + 1) // 2).astype(jnp.int32)
        lane = block - lax.div(row * (row + 1), 2)
        left = panels_ref[:, pl.ds(pl.multiple_of(row * LANES, LANES), LANES)]
        right = panels_ref[:, pl.ds(pl.multiple_of(lane * LANES, LANES), LANES)]
        blocks_ref[n * LANES : (n + 1) * LANES, :] = dot(left, right, ((0,), (0,)))
    offset = pl.multiple_of(start - first * LANES, SUBS)
    tile_ref[...] = blocks_ref[pl.ds(offset, height), :]


def gram_tile(near, far):
    half, part, both = near.shape
    height = len(lower_blocks(both)) * LANES // (2 * half)
    return pl.pallas_call(
        tile_kernel,
        out_shape=(shape(2 * half * part, both), shape(height, LANES)),
        in_specs=[VMEM, VMEM],
        out_specs=(VMEM, VMEM),
        scratch_shapes=[pltpu.VMEM((2 * LANES, LANES), F32)],
        compiler_params=KERNEL,
        cost_estimate=cost(2_200_000_000, 1000),
        name="tile",
    )(near, far)


def row_of(x, i):
    return jnp.broadcast_to(x[i : i + 1, :], (SUBS, LANES))


def column_of(x, j):
    return jnp.broadcast_to(x[:, j : j + 1], (SUBS, LANES))


def combined(weights, rows):
    p = [w * r for w, r in zip(weights, rows)]
    return ((p[0] + p[1]) + (p[2] + p[3])) + ((p[4] + p[5]) + (p[6] + p[7]))


def factor_inverse(lo, a_ref, out_ref):
    hi = lo + LANES
    steps = LANES // SUBS
    lane = lax.broadcasted_iota(jnp.int32, (SUBS, LANES), 1)
    sub = lax.broadcasted_iota(jnp.int32, (SUBS, LANES), 0)
    z = [a_ref[lo + SUBS * i : lo + SUBS * (i + 1), lo:hi] for i in range(steps)]
    for s in range(steps):
        x = [column_of(z[s], SUBS * s + k) for k in range(SUBS)]
        block = (lane >= SUBS * s) & (lane < SUBS * (s + 1))
        slab = jnp.where(block, jnp.where(lane == sub + SUBS * s, 1.0, 0.0), z[s])
        out = jnp.zeros((SUBS, LANES), F32)
        for j in range(SUBS):
            here = sub == j
            pivot = row_of(x[j], j)
            reciprocal = 1.0 / pivot
            for k in range(j + 1, SUBS):
                b = row_of(x[k], j) * reciprocal
                x[k] = jnp.where(here, b, x[k] - x[j] * b)
            row = row_of(slab, j)
            out = jnp.where(here, lax.rsqrt(pivot) * row, out)
            row = row * reciprocal
            slab = jnp.where(here, row, slab - x[j] * row)
        out_ref[lo + SUBS * s : lo + SUBS * (s + 1), lo:hi] = jnp.where(
            lane < SUBS * (s + 1), out, 0.0
        )
        if s + 1 < steps:
            c = [column_of(z[s + 1], SUBS * s + k) for k in range(SUBS)]
            change = combined(c, [row_of(slab, k) for k in range(SUBS)])
            z[s + 1] = jnp.where(block, 0.0, z[s + 1]) - change
        if s + 2 < steps:
            below = jnp.concatenate(z[s + 2 :], axis=0)
            around = [jnp.zeros((SUBS, LANES), F32)] * steps
            around[s] = slab
            change = dot(below, jnp.concatenate(around, axis=0), ((1,), (0,)))
            for i in range(s + 2, steps):
                at = SUBS * (i - s - 2)
                z[i] = jnp.where(block, 0.0, z[i]) - change[at : at + SUBS, :]


def stage_kernel(lo, *refs):
    if lo == 0:
        near_ref, far_ref, a_ref, out_ref, packed_ref = refs
        size = a_ref.shape[0]
        me = lax.axis_index("col")
        half, height, _ = near_ref.shape
        for i in range(half):
            for ref, k in ((near_ref, 2 * i), (far_ref, 2 * i + 1)):
                at = pl.multiple_of(lax.bitwise_xor(me, k) * height, SUBS)
                packed_ref[pl.ds(at, height), :] = ref[i]
        a_ref[...] = jnp.zeros_like(a_ref)
        out_ref[...] = jnp.zeros_like(out_ref)
        for n, (i, j) in enumerate(lower_blocks(size)):
            a_ref[i * LANES : (i + 1) * LANES, j * LANES : (j + 1) * LANES] = packed_ref[
                n * LANES : (n + 1) * LANES, :
            ]
    else:
        a_ref, out_ref = refs[-2:]
        size = a_ref.shape[0]
    hi = lo + LANES
    factor_inverse(lo, a_ref, out_ref)
    inv = out_ref[lo:hi, lo:hi]
    if lo > 0:
        out_ref[lo:hi, :lo] = dot(inv, out_ref[lo:hi, :lo], ((1,), (0,)))
    if hi < size:
        below = dot(a_ref[hi:, lo:hi], inv, ((1,), (1,)))
        a_ref[hi:, hi:] = a_ref[hi:, hi:] - dot(below, below, ((1,), (1,)))
        out_ref[hi:, :hi] = out_ref[hi:, :hi] - dot(below, out_ref[lo:hi, :hi], ((1,), (0,)))


def stage(lo, state, after=()):
    size = 2 * PANEL
    rows = len(lower_blocks(size)) * LANES
    return pl.pallas_call(
        lambda *refs: stage_kernel(lo, *refs),
        out_shape=(shape(size, size), shape(size, size)),
        in_specs=[VMEM, VMEM] + [ANY] * len(after),
        out_specs=(VMEM, VMEM),
        input_output_aliases={0: 0, 1: 1} if lo > 0 else {},
        scratch_shapes=[pltpu.VMEM((rows, LANES), F32)] if lo == 0 else [],
        compiler_params=KERNEL,
        cost_estimate=cost(1000, 1000),
        name="stage",
    )(*state, *after)


def stack_kernel(count, *refs):
    for i in range(count):
        refs[-1][i] = refs[i][...]


def stack_after(pieces, after):
    return pl.pallas_call(
        lambda *refs: stack_kernel(len(pieces), *refs),
        out_shape=shape(len(pieces), *pieces[0].shape),
        in_specs=[VMEM] * len(pieces) + [ANY] * len(after),
        out_specs=VMEM,
        compiler_params=KERNEL,
        cost_estimate=cost(1000, 1000),
        name="stack",
    )(*pieces, *after)


def multiply_kernel(panels_ref, front_ref, *refs):
    out_ref, held_ref, sems = refs[-3:]
    count, _, width = out_ref.shape
    step = max(width, PANEL)
    copies = []
    for lane in range(0, count * width, step):
        product = dot(panels_ref[...], front_ref[:, lane : lane + step], ((0,), (0,)))
        for at in range(0, step, width):
            n = (lane + at) // width
            held_ref[n] = product[:, at : at + width]
            copies.append(pltpu.make_async_copy(held_ref.at[n], out_ref.at[n], sems.at[n]))
            copies[-1].start()
    for copy in copies:
        copy.wait()


def multiply(panels, front, count, after):
    both = panels.shape[1]
    part = (count, both, front.shape[1] // count)
    return pl.pallas_call(
        multiply_kernel,
        out_shape=shape(*part),
        in_specs=[VMEM, VMEM] + [ANY] * len(after),
        out_specs=ANY,
        scratch_shapes=[pltpu.VMEM(part, F32), pltpu.SemaphoreType.DMA((count,))],
        compiler_params=KERNEL,
        cost_estimate=cost(1000, 1000),
        name="multiply",
    )(panels, front, *after)


def hold(array, after):
    return pl.pallas_call(
        lambda *refs: None,
        out_shape=shape(*array.shape),
        in_specs=[ANY] * (1 + len(after)),
        out_specs=ANY,
        input_output_aliases={0: 0},
        compiler_params=KERNEL,
        cost_estimate=cost(1000, 1000),
        name="hold",
    )(array, *after)


def total_kernel(parts_ref, out_ref):
    total = parts_ref[0]
    for i in range(1, parts_ref.shape[0]):
        total = total + parts_ref[i]
    out_ref[...] = total


def total_of(parts):
    return pl.pallas_call(
        total_kernel,
        out_shape=shape(*parts.shape[1:]),
        in_specs=[VMEM],
        out_specs=VMEM,
        compiler_params=KERNEL,
        cost_estimate=cost(1000, 1000),
        name="total",
    )(parts)


def finish_kernel(masks, inv_ref, basis_ref, front_ref, *refs):
    upper_ref, trail_ref, m_ref, w_ref, f_ref, sems = refs[-6:]
    owners, two, part, total = front_ref.shape
    both = inv_ref.shape[0]
    width = refs[0].shape[1]
    columns = []
    for n, mask in enumerate(masks):
        m_ref[:, n * width : (n + 1) * width] = refs[n][...]
        if width == total:
            columns.append(pl.ds(0, width))
        else:
            at = lax.bitwise_xor(lax.axis_index("row"), mask) * width
            columns.append(pl.ds(pl.multiple_of(at, LANES), width))
    copies = []
    for step in range(both // LANES):
        lo, hi = step * LANES, (step + 1) * LANES
        w_ref[lo:hi, :] = dot(inv_ref[lo:hi, :hi], m_ref[:hi, :], ((1,), (0,)))
        for n in range(len(masks)):
            held = w_ref.at[lo:hi, pl.ds(n * width, width)]
            goal = upper_ref.at[lo:hi, columns[n]]
            copies.append(pltpu.make_async_copy(held, goal, sems.at[0, n, step]))
            copies[-1].start()
    rows = LANES // two
    held_owners = rows // part
    for step in range(owners // held_owners):
        lo = step * LANES
        product = dot(basis_ref[lo : lo + LANES, :], w_ref[...], ((1,), (0,)))
        for n in range(len(masks)):
            for owner in range(held_owners):
                for child in range(two):
                    row = (owner * two + child) * part
                    at = step * rows + owner * part
                    f_ref[n, child, at : at + part, :] = (
                        front_ref[step * held_owners + owner, child, :, columns[n]]
                        - product[row : row + part, n * width : (n + 1) * width]
                    )
            held = f_ref.at[n, :, pl.ds(step * rows, rows), :]
            goal = trail_ref.at[:, pl.ds(step * rows, rows), columns[n]]
            copies.append(pltpu.make_async_copy(held, goal, sems.at[1, n, step]))
            copies[-1].start()
    for copy in copies:
        copy.wait()


def finish(pieces, inv, basis, front, given):
    owners, two, part, total = front.shape
    masks = [mask for mask, _ in pieces]
    arrays = [array for _, array in pieces]
    count = len(pieces)
    both, width = arrays[0].shape
    return pl.pallas_call(
        lambda *refs: finish_kernel(masks, *refs),
        out_shape=(shape(both, total), shape(two, owners * part, total)),
        in_specs=[VMEM] * (3 + count) + [ANY] * len(given),
        out_specs=(ANY, ANY),
        input_output_aliases={3 + count: 0, 4 + count: 1} if given else {},
        scratch_shapes=[
            pltpu.VMEM((both, count * width), F32),
            pltpu.VMEM((both, count * width), F32),
            pltpu.VMEM((count, two, owners * part, width), F32),
            pltpu.SemaphoreType.DMA((2, count, both // LANES)),
        ],
        compiler_params=KERNEL,
        cost_estimate=cost(1000, 1000),
        name="finish",
    )(inv, basis, front, *arrays, *given)


def pairs_xor(size, mask):
    return [(i, i ^ mask) for i in range(size)]


def even_pieces(piece, size):
    return [piece] + [lax.ppermute(piece, "col", pairs_xor(size, k)) for k in range(2, size, 2)]


def gather_col(piece, size):
    near = jnp.stack(even_pieces(piece, size))
    return near, lax.ppermute(near, "col", pairs_xor(size, 1))


def sum_row_small(value, size):
    span = 2
    while span <= size:
        value = value + lax.ppermute(value, "row", pairs_xor(size, span - 1))
        span *= 2
    return value


def per_device(children, block_maps):
    cols = lax.axis_size("col")
    rows = lax.axis_size("row")
    rows_dev, width = children.shape[1], children.shape[2]
    blocks_dev = width // PANEL
    part = rows_dev // cols
    both = 2 * PANEL

    spread = lax.all_to_all(pack(children, cols), "col", 0, 0, tiled=True)
    ordered, mine = order(spread, block_maps)
    pieces = even_pieces(mine, cols)
    front = lax.all_to_all(ordered, "col", 0, 0, tiled=True)
    near = stack_after(pieces, [])
    panels, tile = gram_tile(near, lax.ppermute(near, "col", pairs_xor(cols, 1)))
    tile = sum_row_small(tile, rows)
    tiles = even_pieces(tile, cols)

    flat = front.reshape(cols * 2 * part, width)
    products = multiply(panels, flat, rows, [tile])
    parts = lax.all_to_all(products, "row", 0, 0, tiled=True)
    near = stack_after(tiles, [products])
    state = near, lax.ppermute(near, "col", pairs_xor(cols, 1))
    for lo in range(0, both - LANES, LANES):
        state = stage(lo, state)
    mine = total_of(parts)
    _, inv = stage(both - LANES, state, [mine])
    basis = dot(panels, inv, ((1,), (1,)))
    masks = sorted(range(1, rows), key=lambda k: (k.bit_length(), -k))
    pieces = [(0, mine)]
    pieces += [(k, lax.ppermute(mine, "row", pairs_xor(rows, k))) for k in masks]
    if mine.shape[1] % LANES:
        place = lax.axis_index("row")
        ordered = jnp.stack([piece for _, piece in sorted(pieces, key=lambda p: p[0])])
        ordered = jnp.take(ordered, jnp.arange(rows, dtype=jnp.int32) ^ place, axis=0)
        pieces = [(0, ordered.transpose(1, 0, 2).reshape(both, width))]
    outs = ()
    for n in range(0, len(pieces), 2):
        outs = finish(pieces[n : n + 2], inv, basis, front, outs)
    return outs


def solution(mesh):
    placed = (P(None, "row", "col"), P())
    return jax.shard_map(
        per_device,
        mesh=mesh,
        in_specs=placed,
        out_specs=(P(None, "col"), P(None, "row", "col")),
        check_vma=False,
    )
```

```python
import jax
import jax.numpy as jnp
from jax import lax
from jax.experimental import pallas as pl
from jax.experimental.pallas import tpu as pltpu
from jax.sharding import PartitionSpec as P

PANEL = 256
LANES = 128
SUBS = 8
ANY = pl.BlockSpec(memory_space=pl.ANY)
VMEM = pl.BlockSpec(memory_space=pltpu.VMEM)
SMEM = pl.BlockSpec(memory_space=pltpu.SMEM)
KERNEL = pltpu.CompilerParams(vmem_limit_bytes=24 << 20)
F32 = jnp.float32


def dot(left, right, contract):
    return lax.dot_general(
        left,
        right,
        (contract, ((), ())),
        precision=lax.Precision.HIGHEST,
        preferred_element_type=F32,
    )


def shape(*dims):
    return jax.ShapeDtypeStruct(dims, F32)


def cost(flops, size):
    return pl.CostEstimate(flops=flops, bytes_accessed=size, transcendentals=0)


def run_copies(copies):
    for copy in copies:
        copy.start()
    for copy in copies:
        copy.wait()


def pack_kernel(children_ref, out_ref, sems):
    parts, _, part, _ = out_ref.shape
    run_copies(
        [
            pltpu.make_async_copy(
                children_ref.at[:, pl.ds(part * d, part), :], out_ref.at[d], sems.at[d]
            )
            for d in range(parts)
        ]
    )


def pack(children, parts):
    two, rows_dev, width = children.shape
    return pl.pallas_call(
        pack_kernel,
        out_shape=shape(parts, two, rows_dev // parts, width),
        in_specs=[ANY],
        out_specs=ANY,
        scratch_shapes=[pltpu.SemaphoreType.DMA((parts,))],
        compiler_params=KERNEL,
        cost_estimate=cost(1000, 1000),
    )(children)


def order_kernel(maps_ref, spread_ref, out_ref, mine_ref):
    owners, _, part, width = out_ref.shape
    per = width // PANEL
    for child in range(2):
        for block in range(owners * per):
            to = maps_ref[child, block]
            lane = pl.multiple_of(lax.rem(to, per) * PANEL, PANEL)
            from_lane = block % per * PANEL
            out_ref[lax.div(to, per), child, :, pl.ds(lane, PANEL)] = spread_ref[
                block // per, child, :, from_lane : from_lane + PANEL
            ]
        mine_ref[child * part : (child + 1) * part, :] = out_ref[0, child]


def order(spread, maps):
    part, width = spread.shape[2:]
    return pl.pallas_call(
        order_kernel,
        out_shape=(shape(*spread.shape), shape(2 * part, width)),
        in_specs=[SMEM, VMEM],
        out_specs=(VMEM, VMEM),
        compiler_params=KERNEL,
        cost_estimate=cost(1000, 1000),
        name="order",
    )(maps, spread)


def lower_blocks(size):
    return [(i, j) for i in range(size // LANES) for j in range(i + 1)]


def tile_kernel(near_ref, far_ref, panels_ref, tile_ref, blocks_ref):
    me = lax.axis_index("col")
    half, part, both = near_ref.shape
    height = tile_ref.shape[0]
    for i in range(half):
        for ref, k in ((near_ref, 2 * i), (far_ref, 2 * i + 1)):
            at = pl.multiple_of(lax.bitwise_xor(me, k) * part, part)
            panels_ref[pl.ds(at, part), :] = ref[i]
    last = len(lower_blocks(both)) - 1
    start = me * height
    first = lax.div(start, LANES)
    for n in range(2):
        block = lax.min(first + n, last)
        row = jnp.int32(0)
        for i in range(1, both // LANES):
            row = row + (block >= i * (i + 1) // 2).astype(jnp.int32)
        lane = block - lax.div(row * (row + 1), 2)
        left = panels_ref[:, pl.ds(pl.multiple_of(row * LANES, LANES), LANES)]
        right = panels_ref[:, pl.ds(pl.multiple_of(lane * LANES, LANES), LANES)]
        blocks_ref[n * LANES : (n + 1) * LANES, :] = dot(left, right, ((0,), (0,)))
    offset = pl.multiple_of(start - first * LANES, SUBS)
    tile_ref[...] = blocks_ref[pl.ds(offset, height), :]


def gram_tile(near, far):
    half, part, both = near.shape
    height = len(lower_blocks(both)) * LANES // (2 * half)
    return pl.pallas_call(
        tile_kernel,
        out_shape=(shape(2 * half * part, both), shape(height, LANES)),
        in_specs=[VMEM, VMEM],
        out_specs=(VMEM, VMEM),
        scratch_shapes=[pltpu.VMEM((2 * LANES, LANES), F32)],
        compiler_params=KERNEL,
        cost_estimate=cost(2_200_000_000, 1000),
        name="tile",
    )(near, far)


def row_of(x, i):
    return jnp.broadcast_to(x[i : i + 1, :], (SUBS, LANES))


def column_of(x, j):
    return jnp.broadcast_to(x[:, j : j + 1], (SUBS, LANES))


def combined(weights, rows):
    p = [w * r for w, r in zip(weights, rows)]
    return ((p[0] + p[1]) + (p[2] + p[3])) + ((p[4] + p[5]) + (p[6] + p[7]))


def factor_inverse(lo, a_ref, out_ref):
    hi = lo + LANES
    steps = LANES // SUBS
    lane = lax.broadcasted_iota(jnp.int32, (SUBS, LANES), 1)
    sub = lax.broadcasted_iota(jnp.int32, (SUBS, LANES), 0)
    z = [a_ref[lo + SUBS * i : lo + SUBS * (i + 1), lo:hi] for i in range(steps)]
    for s in range(steps):
        x = [column_of(z[s], SUBS * s + k) for k in range(SUBS)]
        block = (lane >= SUBS * s) & (lane < SUBS * (s + 1))
        slab = jnp.where(block, jnp.where(lane == sub + SUBS * s, 1.0, 0.0), z[s])
        out = jnp.zeros((SUBS, LANES), F32)
        for j in range(SUBS):
            here = sub == j
            pivot = row_of(x[j], j)
            reciprocal = 1.0 / pivot
            for k in range(j + 1, SUBS):
                b = row_of(x[k], j) * reciprocal
                x[k] = jnp.where(here, b, x[k] - x[j] * b)
            row = row_of(slab, j)
            out = jnp.where(here, lax.rsqrt(pivot) * row, out)
            row = row * reciprocal
            slab = jnp.where(here, row, slab - x[j] * row)
        out_ref[lo + SUBS * s : lo + SUBS * (s + 1), lo:hi] = jnp.where(
            lane < SUBS * (s + 1), out, 0.0
        )
        if s + 1 < steps:
            c = [column_of(z[s + 1], SUBS * s + k) for k in range(SUBS)]
            change = combined(c, [row_of(slab, k) for k in range(SUBS)])
            z[s + 1] = jnp.where(block, 0.0, z[s + 1]) - change
        if s + 2 < steps:
            below = jnp.concatenate(z[s + 2 :], axis=0)
            around = [jnp.zeros((SUBS, LANES), F32)] * steps
            around[s] = slab
            change = dot(below, jnp.concatenate(around, axis=0), ((1,), (0,)))
            for i in range(s + 2, steps):
                at = SUBS * (i - s - 2)
                z[i] = jnp.where(block, 0.0, z[i]) - change[at : at + SUBS, :]


def stage_kernel(lo, *refs):
    if lo == 0:
        near_ref, far_ref, a_ref, out_ref, packed_ref = refs
        size = a_ref.shape[0]
        me = lax.axis_index("col")
        half, height, _ = near_ref.shape
        for i in range(half):
            for ref, k in ((near_ref, 2 * i), (far_ref, 2 * i + 1)):
                at = pl.multiple_of(lax.bitwise_xor(me, k) * height, SUBS)
                packed_ref[pl.ds(at, height), :] = ref[i]
        a_ref[...] = jnp.zeros_like(a_ref)
        out_ref[...] = jnp.zeros_like(out_ref)
        for n, (i, j) in enumerate(lower_blocks(size)):
            a_ref[i * LANES : (i + 1) * LANES, j * LANES : (j + 1) * LANES] = packed_ref[
                n * LANES : (n + 1) * LANES, :
            ]
    else:
        a_ref, out_ref = refs[-2:]
        size = a_ref.shape[0]
    hi = lo + LANES
    factor_inverse(lo, a_ref, out_ref)
    inv = out_ref[lo:hi, lo:hi]
    if lo > 0:
        out_ref[lo:hi, :lo] = dot(inv, out_ref[lo:hi, :lo], ((1,), (0,)))
    if hi < size:
        below = dot(a_ref[hi:, lo:hi], inv, ((1,), (1,)))
        a_ref[hi:, hi:] = a_ref[hi:, hi:] - dot(below, below, ((1,), (1,)))
        out_ref[hi:, :hi] = out_ref[hi:, :hi] - dot(below, out_ref[lo:hi, :hi], ((1,), (0,)))


def stage(lo, state, after=()):
    size = 2 * PANEL
    rows = len(lower_blocks(size)) * LANES
    return pl.pallas_call(
        lambda *refs: stage_kernel(lo, *refs),
        out_shape=(shape(size, size), shape(size, size)),
        in_specs=[VMEM, VMEM] + [ANY] * len(after),
        out_specs=(VMEM, VMEM),
        input_output_aliases={0: 0, 1: 1} if lo > 0 else {},
        scratch_shapes=[pltpu.VMEM((rows, LANES), F32)] if lo == 0 else [],
        compiler_params=KERNEL,
        cost_estimate=cost(1000, 1000),
        name="stage",
    )(*state, *after)


def stack_kernel(count, *refs):
    for i in range(count):
        refs[-1][i] = refs[i][...]


def stack_after(pieces, after):
    return pl.pallas_call(
        lambda *refs: stack_kernel(len(pieces), *refs),
        out_shape=shape(len(pieces), *pieces[0].shape),
        in_specs=[VMEM] * len(pieces) + [ANY] * len(after),
        out_specs=VMEM,
        compiler_params=KERNEL,
        cost_estimate=cost(1000, 1000),
        name="stack",
    )(*pieces, *after)


def turn_kernel(panels_ref, out_ref):
    out_ref[...] = panels_ref[...].T


def turned(panels):
    return pl.pallas_call(
        turn_kernel,
        out_shape=shape(*panels.shape[::-1]),
        in_specs=[VMEM],
        out_specs=VMEM,
        compiler_params=KERNEL,
        cost_estimate=cost(1000, 1000),
        name="turn",
    )(panels)


def add_kernel(left_ref, right_ref, *refs):
    refs[-1][...] = left_ref[...] + right_ref[...]


def add_after(left, right, after):
    return pl.pallas_call(
        add_kernel,
        out_shape=shape(*left.shape),
        in_specs=[VMEM, VMEM] + [ANY] * len(after),
        out_specs=VMEM,
        compiler_params=KERNEL,
        cost_estimate=cost(1000, 1000),
        name="add",
    )(left, right, *after)


def multiply_kernel(turned_ref, front_ref, *refs):
    out_ref, held_ref, sems = refs[-3:]
    count, _, width = out_ref.shape
    step = max(width, PANEL)
    copies = []
    for lane in range(0, count * width, step):
        product = dot(turned_ref[...], front_ref[:, lane : lane + step], ((1,), (0,)))
        for at in range(0, step, width):
            n = (lane + at) // width
            held_ref[n] = product[:, at : at + width]
            copies.append(pltpu.make_async_copy(held_ref.at[n], out_ref.at[n], sems.at[n]))
            copies[-1].start()
    for copy in copies:
        copy.wait()


def multiply(turned_panels, front, count, after):
    both = turned_panels.shape[0]
    part = (count, both, front.shape[1] // count)
    return pl.pallas_call(
        multiply_kernel,
        out_shape=shape(*part),
        in_specs=[VMEM, VMEM] + [ANY] * len(after),
        out_specs=ANY,
        scratch_shapes=[pltpu.VMEM(part, F32), pltpu.SemaphoreType.DMA((count,))],
        compiler_params=KERNEL,
        cost_estimate=cost(1000, 1000),
        name="multiply",
    )(turned_panels, front, *after)


def hold(array, after):
    return pl.pallas_call(
        lambda *refs: None,
        out_shape=shape(*array.shape),
        in_specs=[ANY] * (1 + len(after)),
        out_specs=ANY,
        input_output_aliases={0: 0},
        compiler_params=KERNEL,
        cost_estimate=cost(1000, 1000),
        name="hold",
    )(array, *after)


def total_kernel(parts_ref, *refs):
    out_ref = refs[-1]
    total = parts_ref[0]
    for i in range(1, parts_ref.shape[0]):
        total = total + parts_ref[i]
    out_ref[...] = total


def total_of(parts, after):
    return pl.pallas_call(
        total_kernel,
        out_shape=shape(*parts.shape[1:]),
        in_specs=[VMEM] + [ANY] * len(after),
        out_specs=VMEM,
        compiler_params=KERNEL,
        cost_estimate=cost(1000, 1000),
        name="total",
    )(parts, *after)


def finish_kernel(masks, inv_ref, basis_ref, front_ref, *refs):
    upper_ref, trail_ref, m_ref, w_ref, f_ref, sems = refs[-6:]
    owners, two, part, total = front_ref.shape
    both = inv_ref.shape[0]
    width = refs[0].shape[1]
    columns = []
    for n, mask in enumerate(masks):
        m_ref[:, n * width : (n + 1) * width] = refs[n][...]
        if width == total:
            columns.append(pl.ds(0, width))
        else:
            at = lax.bitwise_xor(lax.axis_index("row"), mask) * width
            columns.append(pl.ds(pl.multiple_of(at, LANES), width))
    copies = []
    for step in range(both // LANES):
        lo, hi = step * LANES, (step + 1) * LANES
        w_ref[lo:hi, :] = dot(inv_ref[lo:hi, :hi], m_ref[:hi, :], ((1,), (0,)))
        for n in range(len(masks)):
            held = w_ref.at[lo:hi, pl.ds(n * width, width)]
            goal = upper_ref.at[lo:hi, columns[n]]
            copies.append(pltpu.make_async_copy(held, goal, sems.at[0, n, step]))
            copies[-1].start()
    rows = LANES // two
    held_owners = rows // part
    for step in range(owners // held_owners):
        lo = step * LANES
        product = dot(basis_ref[lo : lo + LANES, :], w_ref[...], ((1,), (0,)))
        for n in range(len(masks)):
            for owner in range(held_owners):
                for child in range(two):
                    row = (owner * two + child) * part
                    at = step * rows + owner * part
                    f_ref[n, child, at : at + part, :] = (
                        front_ref[step * held_owners + owner, child, :, columns[n]]
                        - product[row : row + part, n * width : (n + 1) * width]
                    )
            held = f_ref.at[n, :, pl.ds(step * rows, rows), :]
            goal = trail_ref.at[:, pl.ds(step * rows, rows), columns[n]]
            copies.append(pltpu.make_async_copy(held, goal, sems.at[1, n, step]))
            copies[-1].start()
    for copy in copies:
        copy.wait()


def finish(pieces, inv, basis, front, given):
    owners, two, part, total = front.shape
    masks = [mask for mask, _ in pieces]
    arrays = [array for _, array in pieces]
    count = len(pieces)
    both, width = arrays[0].shape
    return pl.pallas_call(
        lambda *refs: finish_kernel(masks, *refs),
        out_shape=(shape(both, total), shape(two, owners * part, total)),
        in_specs=[VMEM] * (3 + count) + [ANY] * len(given),
        out_specs=(ANY, ANY),
        input_output_aliases={3 + count: 0, 4 + count: 1} if given else {},
        scratch_shapes=[
            pltpu.VMEM((both, count * width), F32),
            pltpu.VMEM((both, count * width), F32),
            pltpu.VMEM((count, two, owners * part, width), F32),
            pltpu.SemaphoreType.DMA((2, count, both // LANES)),
        ],
        compiler_params=KERNEL,
        cost_estimate=cost(1000, 1000),
        name="finish",
    )(inv, basis, front, *arrays, *given)


def pairs_xor(size, mask):
    return [(i, i ^ mask) for i in range(size)]


def even_pieces(piece, size):
    return [piece] + [lax.ppermute(piece, "col", pairs_xor(size, k)) for k in range(2, size, 2)]


def gather_col(piece, size):
    near = jnp.stack(even_pieces(piece, size))
    return near, lax.ppermute(near, "col", pairs_xor(size, 1))


def sum_row_small(value, size, after):
    span = 2
    while span < size:
        value = value + lax.ppermute(value, "row", pairs_xor(size, span - 1))
        span *= 2
    return add_after(value, lax.ppermute(value, "row", pairs_xor(size, size - 1)), after)


def per_device(children, block_maps):
    cols = lax.axis_size("col")
    rows = lax.axis_size("row")
    rows_dev, width = children.shape[1], children.shape[2]
    blocks_dev = width // PANEL
    part = rows_dev // cols
    both = 2 * PANEL

    spread = lax.all_to_all(pack(children, cols), "col", 0, 0, tiled=True)
    ordered, mine = order(spread, block_maps)
    pieces = even_pieces(mine, cols)
    front = lax.all_to_all(ordered, "col", 0, 0, tiled=True)
    near = stack_after(pieces, [])
    panels, tile = gram_tile(near, lax.ppermute(near, "col", pairs_xor(cols, 1)))
    across = turned(panels)
    tile = sum_row_small(tile, rows, [across])
    tiles = even_pieces(tile, cols)

    flat = front.reshape(cols * 2 * part, width)
    products = multiply(across, flat, rows, [tile])
    parts = lax.all_to_all(products, "row", 0, 0, tiled=True)
    near = stack_after(tiles, [products])
    state = near, lax.ppermute(near, "col", pairs_xor(cols, 1))
    for lo in range(0, both - LANES, LANES):
        state = stage(lo, state)
    mine = total_of(parts, state[1:])
    _, inv = stage(both - LANES, state, [mine])
    basis = dot(panels, inv, ((1,), (1,)))
    masks = sorted(range(1, rows), key=lambda k: (k.bit_length(), -k))
    pieces = [(0, mine)]
    pieces += [(k, lax.ppermute(mine, "row", pairs_xor(rows, k))) for k in masks]
    if mine.shape[1] % LANES:
        place = lax.axis_index("row")
        ordered = jnp.stack([piece for _, piece in sorted(pieces, key=lambda p: p[0])])
        ordered = jnp.take(ordered, jnp.arange(rows, dtype=jnp.int32) ^ place, axis=0)
        pieces = [(0, ordered.transpose(1, 0, 2).reshape(both, width))]
    outs = ()
    for n in range(0, len(pieces), 2):
        outs = finish(pieces[n : n + 2], inv, basis, front, outs)
    return outs


def solution(mesh):
    placed = (P(None, "row", "col"), P())
    return jax.shard_map(
        per_device,
        mesh=mesh,
        in_specs=placed,
        out_specs=(P(None, "col"), P(None, "row", "col")),
        check_vma=False,
    )
```

```python
import jax
import jax.numpy as jnp
from jax import lax
from jax.experimental import pallas as pl
from jax.experimental.pallas import tpu as pltpu
from jax.sharding import PartitionSpec as P

PANEL = 256
LANES = 128
SUBS = 8
ANY = pl.BlockSpec(memory_space=pl.ANY)
VMEM = pl.BlockSpec(memory_space=pltpu.VMEM)
SMEM = pl.BlockSpec(memory_space=pltpu.SMEM)
KERNEL = pltpu.CompilerParams(vmem_limit_bytes=24 << 20)
F32 = jnp.float32


def dot(left, right, contract):
    return lax.dot_general(
        left,
        right,
        (contract, ((), ())),
        precision=lax.Precision.HIGHEST,
        preferred_element_type=F32,
    )


def shape(*dims):
    return jax.ShapeDtypeStruct(dims, F32)


def cost(flops, size):
    return pl.CostEstimate(flops=flops, bytes_accessed=size, transcendentals=0)


def run_copies(copies):
    for copy in copies:
        copy.start()
    for copy in copies:
        copy.wait()


def pack_kernel(children_ref, out_ref):
    parts, _, part, _ = out_ref.shape
    for d in range(parts):
        out_ref[d] = children_ref[:, d * part : (d + 1) * part, :]


def pack(children, parts):
    two, rows_dev, width = children.shape
    return pl.pallas_call(
        pack_kernel,
        out_shape=shape(parts, two, rows_dev // parts, width),
        in_specs=[VMEM],
        out_specs=VMEM,
        compiler_params=KERNEL,
        cost_estimate=cost(1000, 1000),
        name="pack",
    )(children)


def order_kernel(maps_ref, spread_ref, out_ref, mine_ref):
    owners, _, part, width = out_ref.shape
    per = width // PANEL
    for child in range(2):
        for block in range(owners * per):
            to = maps_ref[child, block]
            lane = pl.multiple_of(lax.rem(to, per) * PANEL, PANEL)
            from_lane = block % per * PANEL
            out_ref[lax.div(to, per), child, :, pl.ds(lane, PANEL)] = spread_ref[
                block // per, child, :, from_lane : from_lane + PANEL
            ]
        mine_ref[child * part : (child + 1) * part, :] = out_ref[0, child]


def order(spread, maps):
    part, width = spread.shape[2:]
    return pl.pallas_call(
        order_kernel,
        out_shape=(shape(*spread.shape), shape(2 * part, width)),
        in_specs=[SMEM, VMEM],
        out_specs=(VMEM, VMEM),
        compiler_params=KERNEL,
        cost_estimate=cost(1000, 1000),
        name="order",
    )(maps, spread)


def lower_blocks(size):
    return [(i, j) for i in range(size // LANES) for j in range(i + 1)]


def tile_kernel(near_ref, far_ref, panels_ref, tile_ref, blocks_ref):
    me = lax.axis_index("col")
    half, part, both = near_ref.shape
    height = tile_ref.shape[0]
    for i in range(half):
        for ref, k in ((near_ref, 2 * i), (far_ref, 2 * i + 1)):
            at = pl.multiple_of(lax.bitwise_xor(me, k) * part, part)
            panels_ref[pl.ds(at, part), :] = ref[i]
    last = len(lower_blocks(both)) - 1
    start = me * height
    first = lax.div(start, LANES)
    for n in range(2):
        block = lax.min(first + n, last)
        row = jnp.int32(0)
        for i in range(1, both // LANES):
            row = row + (block >= i * (i + 1) // 2).astype(jnp.int32)
        lane = block - lax.div(row * (row + 1), 2)
        left = panels_ref[:, pl.ds(pl.multiple_of(row * LANES, LANES), LANES)]
        right = panels_ref[:, pl.ds(pl.multiple_of(lane * LANES, LANES), LANES)]
        blocks_ref[n * LANES : (n + 1) * LANES, :] = dot(left, right, ((0,), (0,)))
    offset = pl.multiple_of(start - first * LANES, SUBS)
    tile_ref[...] = blocks_ref[pl.ds(offset, height), :]


def gram_tile(near, far):
    half, part, both = near.shape
    height = len(lower_blocks(both)) * LANES // (2 * half)
    return pl.pallas_call(
        tile_kernel,
        out_shape=(shape(2 * half * part, both), shape(height, LANES)),
        in_specs=[VMEM, VMEM],
        out_specs=(VMEM, VMEM),
        scratch_shapes=[pltpu.VMEM((2 * LANES, LANES), F32)],
        compiler_params=KERNEL,
        cost_estimate=cost(2_200_000_000, 1000),
        name="tile",
    )(near, far)


def row_of(x, i):
    return jnp.broadcast_to(x[i : i + 1, :], (SUBS, LANES))


def column_of(x, j):
    return jnp.broadcast_to(x[:, j : j + 1], (SUBS, LANES))


def combined(weights, rows):
    p = [w * r for w, r in zip(weights, rows)]
    return ((p[0] + p[1]) + (p[2] + p[3])) + ((p[4] + p[5]) + (p[6] + p[7]))


def factor_inverse(lo, a_ref, out_ref):
    hi = lo + LANES
    steps = LANES // SUBS
    lane = lax.broadcasted_iota(jnp.int32, (SUBS, LANES), 1)
    sub = lax.broadcasted_iota(jnp.int32, (SUBS, LANES), 0)
    z = [a_ref[lo + SUBS * i : lo + SUBS * (i + 1), lo:hi] for i in range(steps)]
    for s in range(steps):
        x = [column_of(z[s], SUBS * s + k) for k in range(SUBS)]
        block = (lane >= SUBS * s) & (lane < SUBS * (s + 1))
        slab = jnp.where(block, jnp.where(lane == sub + SUBS * s, 1.0, 0.0), z[s])
        out = jnp.zeros((SUBS, LANES), F32)
        for j in range(SUBS):
            here = sub == j
            pivot = row_of(x[j], j)
            reciprocal = 1.0 / pivot
            for k in range(j + 1, SUBS):
                b = row_of(x[k], j) * reciprocal
                x[k] = jnp.where(here, b, x[k] - x[j] * b)
            row = row_of(slab, j)
            out = jnp.where(here, lax.rsqrt(pivot) * row, out)
            row = row * reciprocal
            slab = jnp.where(here, row, slab - x[j] * row)
        out_ref[lo + SUBS * s : lo + SUBS * (s + 1), lo:hi] = jnp.where(
            lane < SUBS * (s + 1), out, 0.0
        )
        if s + 1 < steps:
            c = [column_of(z[s + 1], SUBS * s + k) for k in range(SUBS)]
            change = combined(c, [row_of(slab, k) for k in range(SUBS)])
            z[s + 1] = jnp.where(block, 0.0, z[s + 1]) - change
        if s + 2 < steps:
            below = jnp.concatenate(z[s + 2 :], axis=0)
            around = [jnp.zeros((SUBS, LANES), F32)] * steps
            around[s] = slab
            change = dot(below, jnp.concatenate(around, axis=0), ((1,), (0,)))
            for i in range(s + 2, steps):
                at = SUBS * (i - s - 2)
                z[i] = jnp.where(block, 0.0, z[i]) - change[at : at + SUBS, :]


def stage_kernel(lo, *refs):
    if lo == 0:
        near_ref, far_ref, a_ref, out_ref, packed_ref = refs
        size = a_ref.shape[0]
        me = lax.axis_index("col")
        half, height, _ = near_ref.shape
        for i in range(half):
            for ref, k in ((near_ref, 2 * i), (far_ref, 2 * i + 1)):
                at = pl.multiple_of(lax.bitwise_xor(me, k) * height, SUBS)
                packed_ref[pl.ds(at, height), :] = ref[i]
        a_ref[...] = jnp.zeros_like(a_ref)
        out_ref[...] = jnp.zeros_like(out_ref)
        for n, (i, j) in enumerate(lower_blocks(size)):
            a_ref[i * LANES : (i + 1) * LANES, j * LANES : (j + 1) * LANES] = packed_ref[
                n * LANES : (n + 1) * LANES, :
            ]
    else:
        a_ref, out_ref = refs[-2:]
        size = a_ref.shape[0]
    hi = lo + LANES
    factor_inverse(lo, a_ref, out_ref)
    inv = out_ref[lo:hi, lo:hi]
    if lo > 0:
        out_ref[lo:hi, :lo] = dot(inv, out_ref[lo:hi, :lo], ((1,), (0,)))
    if hi < size:
        below = dot(a_ref[hi:, lo:hi], inv, ((1,), (1,)))
        a_ref[hi:, hi:] = a_ref[hi:, hi:] - dot(below, below, ((1,), (1,)))
        out_ref[hi:, :hi] = out_ref[hi:, :hi] - dot(below, out_ref[lo:hi, :hi], ((1,), (0,)))


def stage(lo, state, after=()):
    size = 2 * PANEL
    rows = len(lower_blocks(size)) * LANES
    return pl.pallas_call(
        lambda *refs: stage_kernel(lo, *refs),
        out_shape=(shape(size, size), shape(size, size)),
        in_specs=[VMEM, VMEM] + [ANY] * len(after),
        out_specs=(VMEM, VMEM),
        input_output_aliases={0: 0, 1: 1} if lo > 0 else {},
        scratch_shapes=[pltpu.VMEM((rows, LANES), F32)] if lo == 0 else [],
        compiler_params=KERNEL,
        cost_estimate=cost(1000, 1000),
        name="stage",
    )(*state, *after)


def stack_kernel(count, *refs):
    for i in range(count):
        refs[-1][i] = refs[i][...]


def stack_after(pieces, after):
    return pl.pallas_call(
        lambda *refs: stack_kernel(len(pieces), *refs),
        out_shape=shape(len(pieces), *pieces[0].shape),
        in_specs=[VMEM] * len(pieces) + [ANY] * len(after),
        out_specs=VMEM,
        compiler_params=KERNEL,
        cost_estimate=cost(1000, 1000),
        name="stack",
    )(*pieces, *after)


def turn_kernel(panels_ref, out_ref):
    out_ref[...] = panels_ref[...].T


def turned(panels):
    return pl.pallas_call(
        turn_kernel,
        out_shape=shape(*panels.shape[::-1]),
        in_specs=[VMEM],
        out_specs=VMEM,
        compiler_params=KERNEL,
        cost_estimate=cost(1000, 1000),
        name="turn",
    )(panels)


def add_kernel(left_ref, right_ref, *refs):
    refs[-1][...] = left_ref[...] + right_ref[...]


def add_after(left, right, after):
    return pl.pallas_call(
        add_kernel,
        out_shape=shape(*left.shape),
        in_specs=[VMEM, VMEM] + [ANY] * len(after),
        out_specs=VMEM,
        compiler_params=KERNEL,
        cost_estimate=cost(1000, 1000),
        name="add",
    )(left, right, *after)


def multiply_kernel(turned_ref, front_ref, *refs):
    out_ref, held_ref, sems = refs[-3:]
    count, _, width = out_ref.shape
    step = max(width, PANEL)
    copies = []
    for lane in range(0, count * width, step):
        product = dot(turned_ref[...], front_ref[:, lane : lane + step], ((1,), (0,)))
        for at in range(0, step, width):
            n = (lane + at) // width
            held_ref[n] = product[:, at : at + width]
            copies.append(pltpu.make_async_copy(held_ref.at[n], out_ref.at[n], sems.at[n]))
            copies[-1].start()
    for copy in copies:
        copy.wait()


def multiply(turned_panels, front, count, after):
    both = turned_panels.shape[0]
    part = (count, both, front.shape[1] // count)
    return pl.pallas_call(
        multiply_kernel,
        out_shape=shape(*part),
        in_specs=[VMEM, VMEM] + [ANY] * len(after),
        out_specs=ANY,
        scratch_shapes=[pltpu.VMEM(part, F32), pltpu.SemaphoreType.DMA((count,))],
        compiler_params=KERNEL,
        cost_estimate=cost(1000, 1000),
        name="multiply",
    )(turned_panels, front, *after)


def hold(array, after):
    return pl.pallas_call(
        lambda *refs: None,
        out_shape=shape(*array.shape),
        in_specs=[ANY] * (1 + len(after)),
        out_specs=ANY,
        input_output_aliases={0: 0},
        compiler_params=KERNEL,
        cost_estimate=cost(1000, 1000),
        name="hold",
    )(array, *after)


def total_kernel(parts_ref, *refs):
    out_ref, held_ref, sems = refs[-3:]
    copies = [
        pltpu.make_async_copy(parts_ref.at[n], held_ref.at[n], sems.at[n])
        for n in range(held_ref.shape[0])
    ]
    for copy in copies:
        copy.start()
    copies[0].wait()
    total = held_ref[0]
    for n, copy in enumerate(copies[1:]):
        copy.wait()
        total = total + held_ref[n + 1]
    out_ref[...] = total


def total_of(parts, after):
    return pl.pallas_call(
        total_kernel,
        out_shape=shape(*parts.shape[1:]),
        in_specs=[ANY] * (1 + len(after)),
        out_specs=VMEM,
        scratch_shapes=[
            pltpu.VMEM(parts.shape, F32),
            pltpu.SemaphoreType.DMA(parts.shape[:1]),
        ],
        compiler_params=KERNEL,
        cost_estimate=cost(1000, 1000),
        name="total",
    )(parts, *after)


def finish_kernel(masks, inv_ref, basis_ref, front_ref, *refs):
    upper_ref, trail_ref, m_ref, w_ref, f_ref, sems = refs[-6:]
    owners, two, part, total = front_ref.shape
    both = inv_ref.shape[0]
    width = refs[0].shape[1]
    columns = []
    for n, mask in enumerate(masks):
        m_ref[:, n * width : (n + 1) * width] = refs[n][...]
        if width == total:
            columns.append(pl.ds(0, width))
        else:
            at = lax.bitwise_xor(lax.axis_index("row"), mask) * width
            columns.append(pl.ds(pl.multiple_of(at, LANES), width))
    copies = []
    for step in range(both // LANES):
        lo, hi = step * LANES, (step + 1) * LANES
        w_ref[lo:hi, :] = dot(inv_ref[lo:hi, :hi], m_ref[:hi, :], ((1,), (0,)))
        for n in range(len(masks)):
            held = w_ref.at[lo:hi, pl.ds(n * width, width)]
            goal = upper_ref.at[lo:hi, columns[n]]
            copies.append(pltpu.make_async_copy(held, goal, sems.at[0, n, step]))
            copies[-1].start()
    rows = LANES // two
    held_owners = rows // part
    for step in range(owners // held_owners):
        lo = step * LANES
        product = dot(basis_ref[lo : lo + LANES, :], w_ref[...], ((1,), (0,)))
        for n in range(len(masks)):
            for owner in range(held_owners):
                for child in range(two):
                    row = (owner * two + child) * part
                    at = step * rows + owner * part
                    f_ref[n, child, at : at + part, :] = (
                        front_ref[step * held_owners + owner, child, :, columns[n]]
                        - product[row : row + part, n * width : (n + 1) * width]
                    )
            held = f_ref.at[n, :, pl.ds(step * rows, rows), :]
            goal = trail_ref.at[:, pl.ds(step * rows, rows), columns[n]]
            copies.append(pltpu.make_async_copy(held, goal, sems.at[1, n, step]))
            copies[-1].start()
    for copy in copies:
        copy.wait()


def finish(pieces, inv, basis, front, given):
    owners, two, part, total = front.shape
    masks = [mask for mask, _ in pieces]
    arrays = [array for _, array in pieces]
    count = len(pieces)
    both, width = arrays[0].shape
    return pl.pallas_call(
        lambda *refs: finish_kernel(masks, *refs),
        out_shape=(shape(both, total), shape(two, owners * part, total)),
        in_specs=[VMEM] * (3 + count) + [ANY] * len(given),
        out_specs=(ANY, ANY),
        input_output_aliases={3 + count: 0, 4 + count: 1} if given else {},
        scratch_shapes=[
            pltpu.VMEM((both, count * width), F32),
            pltpu.VMEM((both, count * width), F32),
            pltpu.VMEM((count, two, owners * part, width), F32),
            pltpu.SemaphoreType.DMA((2, count, both // LANES)),
        ],
        compiler_params=KERNEL,
        cost_estimate=cost(1000, 1000),
        name="finish",
    )(inv, basis, front, *arrays, *given)


def pairs_xor(size, mask):
    return [(i, i ^ mask) for i in range(size)]


def even_pieces(piece, size):
    return [piece] + [lax.ppermute(piece, "col", pairs_xor(size, k)) for k in range(2, size, 2)]


def gather_col(piece, size):
    near = jnp.stack(even_pieces(piece, size))
    return near, lax.ppermute(near, "col", pairs_xor(size, 1))


def sum_row_small(value, size, after):
    span = 2
    while span < size:
        value = value + lax.ppermute(value, "row", pairs_xor(size, span - 1))
        span *= 2
    return add_after(value, lax.ppermute(value, "row", pairs_xor(size, size - 1)), after)


def per_device(children, block_maps):
    cols = lax.axis_size("col")
    rows = lax.axis_size("row")
    rows_dev, width = children.shape[1], children.shape[2]
    blocks_dev = width // PANEL
    part = rows_dev // cols
    both = 2 * PANEL

    spread = lax.all_to_all(pack(children, cols), "col", 0, 0, tiled=True)
    ordered, mine = order(spread, block_maps)
    pieces = even_pieces(mine, cols)
    front = lax.all_to_all(ordered, "col", 0, 0, tiled=True)
    near = stack_after(pieces, [])
    panels, tile = gram_tile(near, lax.ppermute(near, "col", pairs_xor(cols, 1)))
    across = turned(panels)
    tile = sum_row_small(tile, rows, [across])
    tiles = even_pieces(tile, cols)

    flat = front.reshape(cols * 2 * part, width)
    products = multiply(across, flat, rows, [tile])
    parts = lax.all_to_all(products, "row", 0, 0, tiled=True)
    near = stack_after(tiles, [products])
    state = near, lax.ppermute(near, "col", pairs_xor(cols, 1))
    for lo in range(0, both - LANES, LANES):
        state = stage(lo, state)
    mine = total_of(parts, state[1:])
    _, inv = stage(both - LANES, state, [mine])
    basis = dot(panels, inv, ((1,), (1,)))
    masks = sorted(range(1, rows), key=lambda k: (k.bit_length(), -k))
    pieces = [(0, mine)]
    pieces += [(k, lax.ppermute(mine, "row", pairs_xor(rows, k))) for k in masks]
    if mine.shape[1] % LANES:
        place = lax.axis_index("row")
        ordered = jnp.stack([piece for _, piece in sorted(pieces, key=lambda p: p[0])])
        ordered = jnp.take(ordered, jnp.arange(rows, dtype=jnp.int32) ^ place, axis=0)
        pieces = [(0, ordered.transpose(1, 0, 2).reshape(both, width))]
    outs = ()
    for n in range(0, len(pieces), 2):
        outs = finish(pieces[n : n + 2], inv, basis, front, outs)
    return outs


def solution(mesh):
    placed = (P(None, "row", "col"), P())
    return jax.shard_map(
        per_device,
        mesh=mesh,
        in_specs=placed,
        out_specs=(P(None, "col"), P(None, "row", "col")),
        check_vma=False,
    )
```

```python
import jax
import jax.numpy as jnp
from jax import lax
from jax.experimental import pallas as pl
from jax.experimental.pallas import tpu as pltpu
from jax.sharding import PartitionSpec as P

PANEL = 256
LANES = 128
SUBS = 8
ANY = pl.BlockSpec(memory_space=pl.ANY)
VMEM = pl.BlockSpec(memory_space=pltpu.VMEM)
SMEM = pl.BlockSpec(memory_space=pltpu.SMEM)
KERNEL = pltpu.CompilerParams(vmem_limit_bytes=24 << 20)
F32 = jnp.float32


def dot(left, right, contract):
    return lax.dot_general(
        left,
        right,
        (contract, ((), ())),
        precision=lax.Precision.HIGHEST,
        preferred_element_type=F32,
    )


def shape(*dims):
    return jax.ShapeDtypeStruct(dims, F32)


def cost(flops, size):
    return pl.CostEstimate(flops=flops, bytes_accessed=size, transcendentals=0)


def run_copies(copies):
    for copy in copies:
        copy.start()
    for copy in copies:
        copy.wait()


def pack_kernel(children_ref, out_ref):
    parts, _, part, _ = out_ref.shape
    for d in range(parts):
        out_ref[d] = children_ref[:, d * part : (d + 1) * part, :]


def pack(children, parts):
    two, rows_dev, width = children.shape
    return pl.pallas_call(
        pack_kernel,
        out_shape=shape(parts, two, rows_dev // parts, width),
        in_specs=[VMEM],
        out_specs=VMEM,
        compiler_params=KERNEL,
        cost_estimate=cost(1000, 1000),
        name="pack",
    )(children)


def order_kernel(maps_ref, spread_ref, out_ref, mine_ref):
    owners, _, part, width = out_ref.shape
    per = width // PANEL
    for child in range(2):
        for block in range(owners * per):
            to = maps_ref[child, block]
            lane = pl.multiple_of(lax.rem(to, per) * PANEL, PANEL)
            from_lane = block % per * PANEL
            out_ref[lax.div(to, per), child, :, pl.ds(lane, PANEL)] = spread_ref[
                block // per, child, :, from_lane : from_lane + PANEL
            ]
        mine_ref[child * part : (child + 1) * part, :] = out_ref[0, child]


def order(spread, maps):
    part, width = spread.shape[2:]
    return pl.pallas_call(
        order_kernel,
        out_shape=(shape(*spread.shape), shape(2 * part, width)),
        in_specs=[SMEM, VMEM],
        out_specs=(VMEM, VMEM),
        compiler_params=KERNEL,
        cost_estimate=cost(1000, 1000),
        name="order",
    )(maps, spread)


def lower_blocks(size):
    return [(i, j) for i in range(size // LANES) for j in range(i + 1)]


def tile_kernel(near_ref, far_ref, panels_ref, tile_ref, blocks_ref):
    me = lax.axis_index("col")
    half, part, both = near_ref.shape
    height = tile_ref.shape[0]
    for i in range(half):
        for ref, k in ((near_ref, 2 * i), (far_ref, 2 * i + 1)):
            at = pl.multiple_of(lax.bitwise_xor(me, k) * part, part)
            panels_ref[pl.ds(at, part), :] = ref[i]
    last = len(lower_blocks(both)) - 1
    start = me * height
    first = lax.div(start, LANES)
    for n in range(2):
        block = lax.min(first + n, last)
        row = jnp.int32(0)
        for i in range(1, both // LANES):
            row = row + (block >= i * (i + 1) // 2).astype(jnp.int32)
        lane = block - lax.div(row * (row + 1), 2)
        left = panels_ref[:, pl.ds(pl.multiple_of(row * LANES, LANES), LANES)]
        right = panels_ref[:, pl.ds(pl.multiple_of(lane * LANES, LANES), LANES)]
        blocks_ref[n * LANES : (n + 1) * LANES, :] = dot(left, right, ((0,), (0,)))
    offset = pl.multiple_of(start - first * LANES, SUBS)
    tile_ref[...] = blocks_ref[pl.ds(offset, height), :]


def gram_tile(near, far):
    half, part, both = near.shape
    height = len(lower_blocks(both)) * LANES // (2 * half)
    return pl.pallas_call(
        tile_kernel,
        out_shape=(shape(2 * half * part, both), shape(height, LANES)),
        in_specs=[VMEM, VMEM],
        out_specs=(VMEM, VMEM),
        scratch_shapes=[pltpu.VMEM((2 * LANES, LANES), F32)],
        compiler_params=KERNEL,
        cost_estimate=cost(2_200_000_000, 1000),
        name="tile",
    )(near, far)


def row_of(x, i):
    return jnp.broadcast_to(x[i : i + 1, :], (SUBS, LANES))


def column_of(x, j):
    return jnp.broadcast_to(x[:, j : j + 1], (SUBS, LANES))


def combined(weights, rows):
    p = [w * r for w, r in zip(weights, rows)]
    return ((p[0] + p[1]) + (p[2] + p[3])) + ((p[4] + p[5]) + (p[6] + p[7]))


def factor_inverse(lo, a_ref, out_ref):
    hi = lo + LANES
    steps = LANES // SUBS
    lane = lax.broadcasted_iota(jnp.int32, (SUBS, LANES), 1)
    sub = lax.broadcasted_iota(jnp.int32, (SUBS, LANES), 0)
    z = [a_ref[lo + SUBS * i : lo + SUBS * (i + 1), lo:hi] for i in range(steps)]
    for s in range(steps):
        x = [column_of(z[s], SUBS * s + k) for k in range(SUBS)]
        block = (lane >= SUBS * s) & (lane < SUBS * (s + 1))
        slab = jnp.where(block, jnp.where(lane == sub + SUBS * s, 1.0, 0.0), z[s])
        out = jnp.zeros((SUBS, LANES), F32)
        for j in range(SUBS):
            here = sub == j
            pivot = row_of(x[j], j)
            reciprocal = 1.0 / pivot
            for k in range(j + 1, SUBS):
                b = row_of(x[k], j) * reciprocal
                x[k] = jnp.where(here, b, x[k] - x[j] * b)
            row = row_of(slab, j)
            out = jnp.where(here, lax.rsqrt(pivot) * row, out)
            row = row * reciprocal
            slab = jnp.where(here, row, slab - x[j] * row)
        out_ref[lo + SUBS * s : lo + SUBS * (s + 1), lo:hi] = jnp.where(
            lane < SUBS * (s + 1), out, 0.0
        )
        if s + 1 < steps:
            c = [column_of(z[s + 1], SUBS * s + k) for k in range(SUBS)]
            change = combined(c, [row_of(slab, k) for k in range(SUBS)])
            z[s + 1] = jnp.where(block, 0.0, z[s + 1]) - change
        if s + 2 < steps:
            below = jnp.concatenate(z[s + 2 :], axis=0)
            around = [jnp.zeros((SUBS, LANES), F32)] * steps
            around[s] = slab
            change = dot(below, jnp.concatenate(around, axis=0), ((1,), (0,)))
            for i in range(s + 2, steps):
                at = SUBS * (i - s - 2)
                z[i] = jnp.where(block, 0.0, z[i]) - change[at : at + SUBS, :]


def stage_kernel(lo, *refs):
    if lo == 0:
        near_ref, far_ref, a_ref, out_ref, packed_ref = refs
        size = a_ref.shape[0]
        me = lax.axis_index("col")
        half, height, _ = near_ref.shape
        for i in range(half):
            for ref, k in ((near_ref, 2 * i), (far_ref, 2 * i + 1)):
                at = pl.multiple_of(lax.bitwise_xor(me, k) * height, SUBS)
                packed_ref[pl.ds(at, height), :] = ref[i]
        a_ref[...] = jnp.zeros_like(a_ref)
        out_ref[...] = jnp.zeros_like(out_ref)
        for n, (i, j) in enumerate(lower_blocks(size)):
            a_ref[i * LANES : (i + 1) * LANES, j * LANES : (j + 1) * LANES] = packed_ref[
                n * LANES : (n + 1) * LANES, :
            ]
    else:
        a_ref, out_ref = refs[-2:]
        size = a_ref.shape[0]
    hi = lo + LANES
    factor_inverse(lo, a_ref, out_ref)
    inv = out_ref[lo:hi, lo:hi]
    if lo > 0:
        out_ref[lo:hi, :lo] = dot(inv, out_ref[lo:hi, :lo], ((1,), (0,)))
    if hi < size:
        below = dot(a_ref[hi:, lo:hi], inv, ((1,), (1,)))
        a_ref[hi:, hi:] = a_ref[hi:, hi:] - dot(below, below, ((1,), (1,)))
        out_ref[hi:, :hi] = out_ref[hi:, :hi] - dot(below, out_ref[lo:hi, :hi], ((1,), (0,)))


def stage(lo, state, after=()):
    size = 2 * PANEL
    rows = len(lower_blocks(size)) * LANES
    return pl.pallas_call(
        lambda *refs: stage_kernel(lo, *refs),
        out_shape=(shape(size, size), shape(size, size)),
        in_specs=[VMEM, VMEM] + [ANY] * len(after),
        out_specs=(VMEM, VMEM),
        input_output_aliases={0: 0, 1: 1} if lo > 0 else {},
        scratch_shapes=[pltpu.VMEM((rows, LANES), F32)] if lo == 0 else [],
        compiler_params=KERNEL,
        cost_estimate=cost(1000, 1000),
        name="stage",
    )(*state, *after)


def stack_kernel(count, *refs):
    for i in range(count):
        refs[-1][i] = refs[i][...]


def stack_after(pieces, after):
    return pl.pallas_call(
        lambda *refs: stack_kernel(len(pieces), *refs),
        out_shape=shape(len(pieces), *pieces[0].shape),
        in_specs=[VMEM] * len(pieces) + [ANY] * len(after),
        out_specs=VMEM,
        compiler_params=KERNEL,
        cost_estimate=cost(1000, 1000),
        name="stack",
    )(*pieces, *after)


def turn_kernel(panels_ref, out_ref):
    out_ref[...] = panels_ref[...].T


def turned(panels):
    return pl.pallas_call(
        turn_kernel,
        out_shape=shape(*panels.shape[::-1]),
        in_specs=[VMEM],
        out_specs=VMEM,
        compiler_params=KERNEL,
        cost_estimate=cost(1000, 1000),
        name="turn",
    )(panels)


def add_kernel(left_ref, right_ref, *refs):
    refs[-1][...] = left_ref[...] + right_ref[...]


def add_after(left, right, after):
    return pl.pallas_call(
        add_kernel,
        out_shape=shape(*left.shape),
        in_specs=[VMEM, VMEM] + [ANY] * len(after),
        out_specs=VMEM,
        compiler_params=KERNEL,
        cost_estimate=cost(1000, 1000),
        name="add",
    )(left, right, *after)


def multiply_kernel(index, turned_ref, front_ref, *refs):
    out_ref, held_ref, sems = refs[-3:]
    count, rows, width = out_ref.shape
    right = front_ref[:, index * width : (index + 1) * width]
    held_ref[...] = dot(turned_ref[...], right, ((1,), (0,)))
    copies = [
        pltpu.make_async_copy(held_ref.at[pl.ds(n * rows, rows)], out_ref.at[n], sems.at[n])
        for n in range(count)
    ]
    for copy in copies:
        copy.start()
    for copy in copies:
        copy.wait()


def multiply(index, turned_panels, front, count, after):
    both = turned_panels.shape[0]
    return pl.pallas_call(
        lambda *refs: multiply_kernel(index, *refs),
        out_shape=shape(count, both // count, PANEL),
        in_specs=[VMEM, VMEM] + [ANY] * len(after),
        out_specs=ANY,
        scratch_shapes=[pltpu.VMEM((both, PANEL), F32), pltpu.SemaphoreType.DMA((count,))],
        compiler_params=KERNEL,
        cost_estimate=cost(1000, 1000),
        name="multiply",
    )(turned_panels, front, *after)


def multiply_apart_kernel(index, masks, turned_ref, front_ref, *refs):
    out_refs, held_ref = refs[-1 - len(masks) : -1], refs[-1]
    rows, width = out_refs[0].shape
    right = front_ref[:, index * width : (index + 1) * width]
    held_ref[...] = dot(turned_ref[...], right, ((1,), (0,)))
    place = lax.axis_index("row")
    for out_ref, mask in zip(out_refs, masks):
        at = pl.multiple_of(lax.bitwise_xor(place, mask) * rows, rows)
        out_ref[...] = held_ref[pl.ds(at, rows), :]


def multiply_apart(index, turned_panels, front, masks, after):
    both = turned_panels.shape[0]
    part = (both // len(masks), PANEL)
    return pl.pallas_call(
        lambda *refs: multiply_apart_kernel(index, masks, *refs),
        out_shape=[shape(*part)] * len(masks),
        in_specs=[VMEM, VMEM] + [ANY] * len(after),
        out_specs=[VMEM] * len(masks),
        scratch_shapes=[pltpu.VMEM((both, PANEL), F32)],
        compiler_params=KERNEL,
        cost_estimate=cost(1000, 1000),
        name="multiply",
    )(turned_panels, front, *after)


def sum_kernel(count, *refs):
    total = refs[0][...]
    for ref in refs[1:count]:
        total = total + ref[...]
    refs[-1][...] = total


def sum_of(parts, after):
    return pl.pallas_call(
        lambda *refs: sum_kernel(len(parts), *refs),
        out_shape=shape(*parts[0].shape),
        in_specs=[VMEM] * len(parts) + [ANY] * len(after),
        out_specs=VMEM,
        compiler_params=KERNEL,
        cost_estimate=cost(1000, 1000),
        name="total",
    )(*parts, *after)


def basis_kernel(panels_ref, inv_ref, *refs):
    refs[-1][...] = dot(panels_ref[...], inv_ref[...], ((1,), (1,)))


def basis_of(panels, inv, after):
    return pl.pallas_call(
        basis_kernel,
        out_shape=shape(*panels.shape),
        in_specs=[VMEM, VMEM] + [ANY] * len(after),
        out_specs=VMEM,
        compiler_params=KERNEL,
        cost_estimate=cost(1000, 1000),
        name="basis",
    )(panels, inv, *after)


def total_kernel(parts_ref, *refs):
    out_ref, held_ref, sems = refs[-3:]
    copies = [
        pltpu.make_async_copy(parts_ref.at[n], held_ref.at[n], sems.at[n])
        for n in range(held_ref.shape[0])
    ]
    for copy in copies:
        copy.start()
    copies[0].wait()
    total = held_ref[0]
    for n, copy in enumerate(copies[1:]):
        copy.wait()
        total = total + held_ref[n + 1]
    out_ref[...] = total


def total_of(parts, after):
    return pl.pallas_call(
        total_kernel,
        out_shape=shape(*parts.shape[1:]),
        in_specs=[ANY] * (1 + len(after)),
        out_specs=VMEM,
        scratch_shapes=[
            pltpu.VMEM(parts.shape, F32),
            pltpu.SemaphoreType.DMA(parts.shape[:1]),
        ],
        compiler_params=KERNEL,
        cost_estimate=cost(1000, 1000),
        name="total",
    )(parts, *after)


def finish_kernel(index, masks, inv_ref, basis_ref, front_ref, *refs):
    upper_ref, trail_ref, m_ref, w_ref, f_ref, sems = refs[-6:]
    owners, two, part, _ = front_ref.shape
    both, width = m_ref.shape
    place = lax.axis_index("row")
    for ref, mask in zip(refs, masks):
        count = ref.shape[0]
        at = pl.multiple_of(lax.bitwise_xor(place, mask) * count, count)
        m_ref[pl.ds(at, count), :] = ref[...]
    columns = pl.ds(index * width, width)
    copies = []
    for step in range(both // LANES):
        lo, hi = step * LANES, (step + 1) * LANES
        w_ref[lo:hi, :] = dot(inv_ref[lo:hi, :hi], m_ref[:hi, :], ((1,), (0,)))
        copies.append(
            pltpu.make_async_copy(w_ref.at[lo:hi], upper_ref.at[lo:hi, columns], sems.at[0, step])
        )
        copies[-1].start()
    rows = LANES // two
    held_owners = rows // part
    for step in range(owners // held_owners):
        lo = step * LANES
        product = dot(basis_ref[lo : lo + LANES, :], w_ref[...], ((1,), (0,)))
        for owner in range(held_owners):
            for child in range(two):
                row = (owner * two + child) * part
                at = step * rows + owner * part
                f_ref[child, at : at + part, :] = (
                    front_ref[step * held_owners + owner, child, :, columns]
                    - product[row : row + part, :]
                )
        held = f_ref.at[:, pl.ds(step * rows, rows), :]
        goal = trail_ref.at[:, pl.ds(step * rows, rows), columns]
        copies.append(pltpu.make_async_copy(held, goal, sems.at[1, step]))
        copies[-1].start()
    for copy in copies:
        copy.wait()


def finish(index, inv, basis, front, masks, pieces, given):
    owners, two, part, total = front.shape
    both, width = inv.shape[0], pieces[0].shape[1]
    taken = 3 + len(pieces)
    return pl.pallas_call(
        lambda *refs: finish_kernel(index, masks, *refs),
        out_shape=(shape(both, total), shape(two, owners * part, total)),
        in_specs=[VMEM] * taken + [ANY] * len(given),
        out_specs=(ANY, ANY),
        input_output_aliases={taken: 0, taken + 1: 1} if given else {},
        scratch_shapes=[
            pltpu.VMEM((both, width), F32),
            pltpu.VMEM((both, width), F32),
            pltpu.VMEM((two, owners * part, width), F32),
            pltpu.SemaphoreType.DMA((2, both // LANES)),
        ],
        compiler_params=KERNEL,
        cost_estimate=cost(1000, 1000),
        name="finish",
    )(inv, basis, front, *pieces, *given)


def pairs_xor(size, mask):
    return [(i, i ^ mask) for i in range(size)]


def even_pieces(piece, size):
    return [piece] + [lax.ppermute(piece, "col", pairs_xor(size, k)) for k in range(2, size, 2)]


def gather_col(piece, size):
    near = jnp.stack(even_pieces(piece, size))
    return near, lax.ppermute(near, "col", pairs_xor(size, 1))


def sum_row_small(value, size, after):
    span = 2
    while span < size:
        value = value + lax.ppermute(value, "row", pairs_xor(size, span - 1))
        span *= 2
    return add_after(value, lax.ppermute(value, "row", pairs_xor(size, size - 1)), after)


def per_device(children, block_maps):
    cols = lax.axis_size("col")
    rows = lax.axis_size("row")
    rows_dev, width = children.shape[1], children.shape[2]
    blocks_dev = width // PANEL
    part = rows_dev // cols
    both = 2 * PANEL

    spread = lax.all_to_all(pack(children, cols), "col", 0, 0, tiled=True)
    ordered, mine = order(spread, block_maps)
    pieces = even_pieces(mine, cols)
    front = lax.all_to_all(ordered, "col", 0, 0, tiled=True)
    near = stack_after(pieces, [])
    panels, tile = gram_tile(near, lax.ppermute(near, "col", pairs_xor(cols, 1)))
    across = turned(panels)
    tile = sum_row_small(tile, rows, [across])
    tiles = even_pieces(tile, cols)

    flat = front.reshape(cols * 2 * part, width)
    masks = sorted(range(rows), key=lambda k: (k.bit_length(), -k))
    products = multiply(0, across, flat, rows, [tile])
    parts = lax.all_to_all(products, "row", 0, 0, tiled=True)
    apart = multiply_apart(1, across, flat, masks, [tile, products])
    rest = [apart[0]] + [
        lax.ppermute(x, "row", pairs_xor(rows, k)) for k, x in zip(masks[1:], apart[1:])
    ]
    near = stack_after(tiles, [products, apart[0]])
    state = near, lax.ppermute(near, "col", pairs_xor(cols, 1))
    state = stage(0, state)
    first = total_of(parts, state[1:])
    state = stage(LANES, state, [first])
    state = stage(2 * LANES, state)
    second = sum_of(rest, state[1:])
    groups = [
        [total] + [lax.ppermute(total, "row", pairs_xor(rows, k)) for k in masks[1:]]
        for total in (first, second)
    ]
    _, inv = stage(3 * LANES, state, [second])
    basis = basis_of(panels, inv, groups[0][1:])
    outs = ()
    for n, pieces in enumerate(groups):
        outs = finish(n, inv, basis, front, masks, pieces, outs)
    return outs


def solution(mesh):
    placed = (P(None, "row", "col"), P())
    return jax.shard_map(
        per_device,
        mesh=mesh,
        in_specs=placed,
        out_specs=(P(None, "col"), P(None, "row", "col")),
        check_vma=False,
    )
```

```python
import jax
import jax.numpy as jnp
from jax import lax
from jax.experimental import pallas as pl
from jax.experimental.pallas import tpu as pltpu
from jax.sharding import PartitionSpec as P

PANEL = 256
LANES = 128
SUBS = 8
ANY = pl.BlockSpec(memory_space=pl.ANY)
VMEM = pl.BlockSpec(memory_space=pltpu.VMEM)
SMEM = pl.BlockSpec(memory_space=pltpu.SMEM)
KERNEL = pltpu.CompilerParams(vmem_limit_bytes=24 << 20)
F32 = jnp.float32


def dot(left, right, contract):
    return lax.dot_general(
        left,
        right,
        (contract, ((), ())),
        precision=lax.Precision.HIGHEST,
        preferred_element_type=F32,
    )


def shape(*dims):
    return jax.ShapeDtypeStruct(dims, F32)


def cost(flops, size):
    return pl.CostEstimate(flops=flops, bytes_accessed=size, transcendentals=0)


def run_copies(copies):
    for copy in copies:
        copy.start()
    for copy in copies:
        copy.wait()


def pack_kernel(children_ref, out_ref):
    parts, _, part, _ = out_ref.shape
    for d in range(parts):
        out_ref[d] = children_ref[:, d * part : (d + 1) * part, :]


def pack(children, parts):
    two, rows_dev, width = children.shape
    return pl.pallas_call(
        pack_kernel,
        out_shape=shape(parts, two, rows_dev // parts, width),
        in_specs=[VMEM],
        out_specs=VMEM,
        compiler_params=KERNEL,
        cost_estimate=cost(1000, 1000),
        name="pack",
    )(children)


def order_kernel(maps_ref, spread_ref, out_ref, mine_ref):
    owners, _, part, width = out_ref.shape
    per = width // PANEL
    for child in range(2):
        for block in range(owners * per):
            to = maps_ref[child, block]
            lane = pl.multiple_of(lax.rem(to, per) * PANEL, PANEL)
            from_lane = block % per * PANEL
            out_ref[lax.div(to, per), child, :, pl.ds(lane, PANEL)] = spread_ref[
                block // per, child, :, from_lane : from_lane + PANEL
            ]
        mine_ref[child * part : (child + 1) * part, :] = out_ref[0, child]


def order(spread, maps):
    part, width = spread.shape[2:]
    return pl.pallas_call(
        order_kernel,
        out_shape=(shape(*spread.shape), shape(2 * part, width)),
        in_specs=[SMEM, VMEM],
        out_specs=(VMEM, VMEM),
        compiler_params=KERNEL,
        cost_estimate=cost(1000, 1000),
        name="order",
    )(maps, spread)


def lower_blocks(size):
    return [(i, j) for i in range(size // LANES) for j in range(i + 1)]


def tile_kernel(near_ref, far_ref, panels_ref, tile_ref, blocks_ref):
    me = lax.axis_index("col")
    half, part, both = near_ref.shape
    height = tile_ref.shape[0]
    for i in range(half):
        for ref, k in ((near_ref, 2 * i), (far_ref, 2 * i + 1)):
            at = pl.multiple_of(lax.bitwise_xor(me, k) * part, part)
            panels_ref[pl.ds(at, part), :] = ref[i]
    last = len(lower_blocks(both)) - 1
    start = me * height
    first = lax.div(start, LANES)
    for n in range(2):
        block = lax.min(first + n, last)
        row = jnp.int32(0)
        for i in range(1, both // LANES):
            row = row + (block >= i * (i + 1) // 2).astype(jnp.int32)
        lane = block - lax.div(row * (row + 1), 2)
        left = panels_ref[:, pl.ds(pl.multiple_of(row * LANES, LANES), LANES)]
        right = panels_ref[:, pl.ds(pl.multiple_of(lane * LANES, LANES), LANES)]
        blocks_ref[n * LANES : (n + 1) * LANES, :] = dot(left, right, ((0,), (0,)))
    offset = pl.multiple_of(start - first * LANES, SUBS)
    tile_ref[...] = blocks_ref[pl.ds(offset, height), :]


def gram_tile(near, far):
    half, part, both = near.shape
    height = len(lower_blocks(both)) * LANES // (2 * half)
    return pl.pallas_call(
        tile_kernel,
        out_shape=(shape(2 * half * part, both), shape(height, LANES)),
        in_specs=[VMEM, VMEM],
        out_specs=(VMEM, VMEM),
        scratch_shapes=[pltpu.VMEM((2 * LANES, LANES), F32)],
        compiler_params=KERNEL,
        cost_estimate=cost(2_200_000_000, 1000),
        name="tile",
    )(near, far)


def row_of(x, i):
    return jnp.broadcast_to(x[i : i + 1, :], (SUBS, LANES))


def column_of(x, j):
    return jnp.broadcast_to(x[:, j : j + 1], (SUBS, LANES))


def combined(weights, rows):
    p = [w * r for w, r in zip(weights, rows)]
    return ((p[0] + p[1]) + (p[2] + p[3])) + ((p[4] + p[5]) + (p[6] + p[7]))


def factor_inverse(lo, a_ref, out_ref):
    hi = lo + LANES
    steps = LANES // SUBS
    lane = lax.broadcasted_iota(jnp.int32, (SUBS, LANES), 1)
    sub = lax.broadcasted_iota(jnp.int32, (SUBS, LANES), 0)
    z = [a_ref[lo + SUBS * i : lo + SUBS * (i + 1), lo:hi] for i in range(steps)]
    for s in range(steps):
        x = [column_of(z[s], SUBS * s + k) for k in range(SUBS)]
        block = (lane >= SUBS * s) & (lane < SUBS * (s + 1))
        slab = jnp.where(block, jnp.where(lane == sub + SUBS * s, 1.0, 0.0), z[s])
        out = jnp.zeros((SUBS, LANES), F32)
        for j in range(SUBS):
            here = sub == j
            pivot = row_of(x[j], j)
            reciprocal = 1.0 / pivot
            for k in range(j + 1, SUBS):
                b = row_of(x[k], j) * reciprocal
                x[k] = jnp.where(here, b, x[k] - x[j] * b)
            row = row_of(slab, j)
            out = jnp.where(here, lax.rsqrt(pivot) * row, out)
            row = row * reciprocal
            slab = jnp.where(here, row, slab - x[j] * row)
        out_ref[lo + SUBS * s : lo + SUBS * (s + 1), lo:hi] = jnp.where(
            lane < SUBS * (s + 1), out, 0.0
        )
        if s + 1 < steps:
            c = [column_of(z[s + 1], SUBS * s + k) for k in range(SUBS)]
            change = combined(c, [row_of(slab, k) for k in range(SUBS)])
            z[s + 1] = jnp.where(block, 0.0, z[s + 1]) - change
        if s + 2 < steps:
            below = jnp.concatenate(z[s + 2 :], axis=0)
            around = [jnp.zeros((SUBS, LANES), F32)] * steps
            around[s] = slab
            change = dot(below, jnp.concatenate(around, axis=0), ((1,), (0,)))
            for i in range(s + 2, steps):
                at = SUBS * (i - s - 2)
                z[i] = jnp.where(block, 0.0, z[i]) - change[at : at + SUBS, :]


def stage_kernel(lo, *refs):
    if lo == 0:
        near_ref, far_ref, a_ref, out_ref, packed_ref = refs
        size = a_ref.shape[0]
        me = lax.axis_index("col")
        half, height, _ = near_ref.shape
        for i in range(half):
            for ref, k in ((near_ref, 2 * i), (far_ref, 2 * i + 1)):
                at = pl.multiple_of(lax.bitwise_xor(me, k) * height, SUBS)
                packed_ref[pl.ds(at, height), :] = ref[i]
        a_ref[...] = jnp.zeros_like(a_ref)
        out_ref[...] = jnp.zeros_like(out_ref)
        for n, (i, j) in enumerate(lower_blocks(size)):
            a_ref[i * LANES : (i + 1) * LANES, j * LANES : (j + 1) * LANES] = packed_ref[
                n * LANES : (n + 1) * LANES, :
            ]
    else:
        a_ref, out_ref = refs[-2:]
        size = a_ref.shape[0]
    hi = lo + LANES
    factor_inverse(lo, a_ref, out_ref)
    inv = out_ref[lo:hi, lo:hi]
    if lo > 0:
        out_ref[lo:hi, :lo] = dot(inv, out_ref[lo:hi, :lo], ((1,), (0,)))
    if hi < size:
        below = dot(a_ref[hi:, lo:hi], inv, ((1,), (1,)))
        a_ref[hi:, hi:] = a_ref[hi:, hi:] - dot(below, below, ((1,), (1,)))
        out_ref[hi:, :hi] = out_ref[hi:, :hi] - dot(below, out_ref[lo:hi, :hi], ((1,), (0,)))


def stage(lo, state, after=()):
    size = 2 * PANEL
    rows = len(lower_blocks(size)) * LANES
    return pl.pallas_call(
        lambda *refs: stage_kernel(lo, *refs),
        out_shape=(shape(size, size), shape(size, size)),
        in_specs=[VMEM, VMEM] + [ANY] * len(after),
        out_specs=(VMEM, VMEM),
        input_output_aliases={0: 0, 1: 1} if lo > 0 else {},
        scratch_shapes=[pltpu.VMEM((rows, LANES), F32)] if lo == 0 else [],
        compiler_params=KERNEL,
        cost_estimate=cost(1000, 1000),
        name="stage",
    )(*state, *after)


def stack_kernel(count, *refs):
    for i in range(count):
        refs[-1][i] = refs[i][...]


def stack_after(pieces, after):
    return pl.pallas_call(
        lambda *refs: stack_kernel(len(pieces), *refs),
        out_shape=shape(len(pieces), *pieces[0].shape),
        in_specs=[VMEM] * len(pieces) + [ANY] * len(after),
        out_specs=VMEM,
        compiler_params=KERNEL,
        cost_estimate=cost(1000, 1000),
        name="stack",
    )(*pieces, *after)


def turn_kernel(panels_ref, out_ref):
    out_ref[...] = panels_ref[...].T


def turned(panels):
    return pl.pallas_call(
        turn_kernel,
        out_shape=shape(*panels.shape[::-1]),
        in_specs=[VMEM],
        out_specs=VMEM,
        compiler_params=KERNEL,
        cost_estimate=cost(1000, 1000),
        name="turn",
    )(panels)


def add_kernel(left_ref, right_ref, *refs):
    refs[-1][...] = left_ref[...] + right_ref[...]


def add_after(left, right, after):
    return pl.pallas_call(
        add_kernel,
        out_shape=shape(*left.shape),
        in_specs=[VMEM, VMEM] + [ANY] * len(after),
        out_specs=VMEM,
        compiler_params=KERNEL,
        cost_estimate=cost(1000, 1000),
        name="add",
    )(left, right, *after)


def multiply_kernel(index, turned_ref, front_ref, *refs):
    out_ref, held_ref, sems = refs[-3:]
    count, rows, width = out_ref.shape
    right = front_ref[:, index * width : (index + 1) * width]
    held_ref[...] = dot(turned_ref[...], right, ((1,), (0,)))
    copies = [
        pltpu.make_async_copy(held_ref.at[pl.ds(n * rows, rows)], out_ref.at[n], sems.at[n])
        for n in range(count)
    ]
    for copy in copies:
        copy.start()
    for copy in copies:
        copy.wait()


def multiply(index, turned_panels, front, count, after):
    both = turned_panels.shape[0]
    return pl.pallas_call(
        lambda *refs: multiply_kernel(index, *refs),
        out_shape=shape(count, both // count, PANEL),
        in_specs=[VMEM, VMEM] + [ANY] * len(after),
        out_specs=ANY,
        scratch_shapes=[pltpu.VMEM((both, PANEL), F32), pltpu.SemaphoreType.DMA((count,))],
        compiler_params=KERNEL,
        cost_estimate=cost(1000, 1000),
        name="multiply",
    )(turned_panels, front, *after)


def multiply_apart_kernel(index, masks, turned_ref, front_ref, *refs):
    out_refs, held_ref = refs[-1 - len(masks) : -1], refs[-1]
    rows, width = out_refs[0].shape
    right = front_ref[:, index * width : (index + 1) * width]
    held_ref[...] = dot(turned_ref[...], right, ((1,), (0,)))
    place = lax.axis_index("row")
    for out_ref, mask in zip(out_refs, masks):
        at = pl.multiple_of(lax.bitwise_xor(place, mask) * rows, rows)
        out_ref[...] = held_ref[pl.ds(at, rows), :]


def multiply_apart(index, turned_panels, front, masks, after):
    both = turned_panels.shape[0]
    part = (both // len(masks), PANEL)
    return pl.pallas_call(
        lambda *refs: multiply_apart_kernel(index, masks, *refs),
        out_shape=[shape(*part)] * len(masks),
        in_specs=[VMEM, VMEM] + [ANY] * len(after),
        out_specs=[VMEM] * len(masks),
        scratch_shapes=[pltpu.VMEM((both, PANEL), F32)],
        compiler_params=KERNEL,
        cost_estimate=cost(1000, 1000),
        name="multiply",
    )(turned_panels, front, *after)


def sum_kernel(count, *refs):
    total = refs[0][...]
    for ref in refs[1:count]:
        total = total + ref[...]
    refs[-1][...] = total


def sum_of(parts, after):
    return pl.pallas_call(
        lambda *refs: sum_kernel(len(parts), *refs),
        out_shape=shape(*parts[0].shape),
        in_specs=[VMEM] * len(parts) + [ANY] * len(after),
        out_specs=VMEM,
        compiler_params=KERNEL,
        cost_estimate=cost(1000, 1000),
        name="total",
    )(*parts, *after)


def basis_kernel(panels_ref, inv_ref, *refs):
    refs[-1][...] = dot(panels_ref[...], inv_ref[...], ((1,), (1,)))


def basis_of(panels, inv, after):
    return pl.pallas_call(
        basis_kernel,
        out_shape=shape(*panels.shape),
        in_specs=[VMEM, VMEM] + [ANY] * len(after),
        out_specs=VMEM,
        compiler_params=KERNEL,
        cost_estimate=cost(1000, 1000),
        name="basis",
    )(panels, inv, *after)


def total_kernel(parts_ref, *refs):
    out_ref, held_ref, sems = refs[-3:]
    copies = [
        pltpu.make_async_copy(parts_ref.at[n], held_ref.at[n], sems.at[n])
        for n in range(held_ref.shape[0])
    ]
    for copy in copies:
        copy.start()
    copies[0].wait()
    total = held_ref[0]
    for n, copy in enumerate(copies[1:]):
        copy.wait()
        total = total + held_ref[n + 1]
    out_ref[...] = total


def total_of(parts, after):
    return pl.pallas_call(
        total_kernel,
        out_shape=shape(*parts.shape[1:]),
        in_specs=[ANY] * (1 + len(after)),
        out_specs=VMEM,
        scratch_shapes=[
            pltpu.VMEM(parts.shape, F32),
            pltpu.SemaphoreType.DMA(parts.shape[:1]),
        ],
        compiler_params=KERNEL,
        cost_estimate=cost(1000, 1000),
        name="total",
    )(parts, *after)


def finish_kernel(index, masks, inv_ref, basis_ref, front_ref, *refs):
    upper_ref, trail_ref, m_ref, w_ref, f_ref, sems = refs[-6:]
    owners, two, part, _ = front_ref.shape
    both, width = m_ref.shape
    place = lax.axis_index("row")
    for ref, mask in zip(refs, masks):
        count = ref.shape[0]
        at = pl.multiple_of(lax.bitwise_xor(place, mask) * count, count)
        m_ref[pl.ds(at, count), :] = ref[...]
    columns = pl.ds(index * width, width)
    copies = []
    for step in range(both // PANEL):
        lo, hi = step * PANEL, (step + 1) * PANEL
        w_ref[lo:hi, :] = dot(inv_ref[lo:hi, :hi], m_ref[:hi, :], ((1,), (0,)))
        copies.append(
            pltpu.make_async_copy(w_ref.at[lo:hi], upper_ref.at[lo:hi, columns], sems.at[0, step])
        )
        copies[-1].start()
    rows = PANEL // two
    held_owners = rows // part
    for step in range(owners // held_owners):
        lo = step * PANEL
        product = dot(basis_ref[lo : lo + PANEL, :], w_ref[...], ((1,), (0,)))
        for owner in range(held_owners):
            for child in range(two):
                row = (owner * two + child) * part
                at = step * rows + owner * part
                f_ref[child, at : at + part, :] = (
                    front_ref[step * held_owners + owner, child, :, columns]
                    - product[row : row + part, :]
                )
        held = f_ref.at[:, pl.ds(step * rows, rows), :]
        goal = trail_ref.at[:, pl.ds(step * rows, rows), columns]
        copies.append(pltpu.make_async_copy(held, goal, sems.at[1, step]))
        copies[-1].start()
    for copy in copies:
        copy.wait()


def finish(index, inv, basis, front, masks, pieces, given):
    owners, two, part, total = front.shape
    both, width = inv.shape[0], pieces[0].shape[1]
    taken = 3 + len(pieces)
    return pl.pallas_call(
        lambda *refs: finish_kernel(index, masks, *refs),
        out_shape=(shape(both, total), shape(two, owners * part, total)),
        in_specs=[VMEM] * taken + [ANY] * len(given),
        out_specs=(ANY, ANY),
        input_output_aliases={taken: 0, taken + 1: 1} if given else {},
        scratch_shapes=[
            pltpu.VMEM((both, width), F32),
            pltpu.VMEM((both, width), F32),
            pltpu.VMEM((two, owners * part, width), F32),
            pltpu.SemaphoreType.DMA((2, both // LANES)),
        ],
        compiler_params=KERNEL,
        cost_estimate=cost(1000, 1000),
        name="finish",
    )(inv, basis, front, *pieces, *given)


def pairs_xor(size, mask):
    return [(i, i ^ mask) for i in range(size)]


def even_pieces(piece, size):
    return [piece] + [lax.ppermute(piece, "col", pairs_xor(size, k)) for k in range(2, size, 2)]


def gather_col(piece, size):
    near = jnp.stack(even_pieces(piece, size))
    return near, lax.ppermute(near, "col", pairs_xor(size, 1))


def sum_row_small(value, size, after):
    span = 2
    while span < size:
        value = value + lax.ppermute(value, "row", pairs_xor(size, span - 1))
        span *= 2
    return add_after(value, lax.ppermute(value, "row", pairs_xor(size, size - 1)), after)


def per_device(children, block_maps):
    cols = lax.axis_size("col")
    rows = lax.axis_size("row")
    rows_dev, width = children.shape[1], children.shape[2]
    blocks_dev = width // PANEL
    part = rows_dev // cols
    both = 2 * PANEL

    spread = lax.all_to_all(pack(children, cols), "col", 0, 0, tiled=True)
    ordered, mine = order(spread, block_maps)
    pieces = even_pieces(mine, cols)
    front = lax.all_to_all(ordered, "col", 0, 0, tiled=True)
    near = stack_after(pieces, [])
    panels, tile = gram_tile(near, lax.ppermute(near, "col", pairs_xor(cols, 1)))
    across = turned(panels)
    tile = sum_row_small(tile, rows, [across])
    tiles = even_pieces(tile, cols)

    flat = front.reshape(cols * 2 * part, width)
    masks = sorted(range(rows), key=lambda k: (k.bit_length(), -k))
    products = multiply(0, across, flat, rows, [tile])
    parts = lax.all_to_all(products, "row", 0, 0, tiled=True)
    apart = multiply_apart(1, across, flat, masks, [tile, products])
    rest = [apart[0]] + [
        lax.ppermute(x, "row", pairs_xor(rows, k)) for k, x in zip(masks[1:], apart[1:])
    ]
    near = stack_after(tiles, [products, apart[0]])
    state = near, lax.ppermute(near, "col", pairs_xor(cols, 1))
    state = stage(0, state)
    first = total_of(parts, state[1:])
    state = stage(LANES, state, [first])
    state = stage(2 * LANES, state)
    second = sum_of(rest, state[1:])
    groups = [
        [total] + [lax.ppermute(total, "row", pairs_xor(rows, k)) for k in masks[1:]]
        for total in (first, second)
    ]
    _, inv = stage(3 * LANES, state, [second])
    basis = basis_of(panels, inv, groups[0][1:])
    outs = ()
    for n, pieces in enumerate(groups):
        outs = finish(n, inv, basis, front, masks, pieces, outs)
    return outs


def solution(mesh):
    placed = (P(None, "row", "col"), P())
    return jax.shard_map(
        per_device,
        mesh=mesh,
        in_specs=placed,
        out_specs=(P(None, "col"), P(None, "row", "col")),
        check_vma=False,
    )
```
